32 devices in a mesh: leaf: 16 (over z, y, x), sub: 2 (over core).
Axes of the slice: x: 2, y: 2, z: 4, core: 2. Of those that a mesh axis runs over, the one named last changes fastest.
Arguments:
- density: bfloat16 [128, 256, 32], P('leaf', None, 'sub'), may hold values from -6 to 6
- near_blocks: bfloat16 [128, 6, 256, 256], P('leaf', 'sub'), may hold values from -0.15625 to 0.15625
- near_index: int32 [128, 6], P('leaf', 'sub'), may hold values from 0 to 127, as said below
- col_basis: bfloat16 [128, 256, 64], P('leaf'), may hold values from -0.375 to 0.375
- row_basis: bfloat16 [128, 256, 64], P('leaf'), may hold values from -0.75 to 0.75
- leaf_coupling: bfloat16 [128, 6, 64, 64], P('leaf', 'sub'), may hold values from -0.3125 to 0.3125
- leaf_list: int32 [128, 6], P('leaf', 'sub'), may hold values from 0 to 127, as said below
- leaf_up: bfloat16 [128, 64, 64], P('leaf'), may hold values from -0.25 to 0.25
- leaf_down: bfloat16 [128, 64, 64], P('leaf'), may hold values from -0.75 to 0.75
- node_coupling: bfloat16 [16, 4, 64, 64], P('leaf'), may hold values from -0.375 to 0.375
- node_list: int32 [16, 4], P('leaf'), may hold values from 0 to 15, as said below
- node_up: bfloat16 [16, 64, 64], P('leaf'), may hold values from -0.5 to 0.5
- node_down: bfloat16 [16, 64, 64], P('leaf'), may hold values from -0.75 to 0.75
- upper_coupling: bfloat16 [14, 4, 64, 64], replicated, may hold values from -0.375 to 0.375
- upper_list: int32 [14, 4], replicated, may hold values from 2 to 15, as said below
- upper_up: bfloat16 [12, 64, 64], replicated, may hold values from -0.5 to 0.5
- upper_down: bfloat16 [12, 64, 64], replicated, may hold values from -0.75 to 0.75
Outputs:
- potential: bfloat16 [128, 256, 32], P('leaf', None, 'sub')
The draws below stay inside these ranges and needn't reach their ends.
Inputs may be any that keep to these rules, and one draw needn't show every extreme that they name: `near_index`: row t holds 6 different leaves, the first being t itself; all lie among the leaves of t's own block of 8 and of the blocks just before and after it; none stands in row t of leaf_list. `leaf_list`: row t holds 6 different leaves other than t, all among the leaves of t's own block of 8 and of the blocks just before and after it. `node_list`: row d holds 4 different clusters other than d; the first is (d + 8) mod 16. `upper_list`: row n - 2 names nodes of node n's level other than n, possibly repeated; the first is the node half that level's size away.
All inputs are finite; a program needn't handle non-finite values.
Results may differ from the reference program's by a relative error of at most 0.029.
Values may be sent and summed in bfloat16 or wider, within the bound.
No kernel may reach another device: no remote copies, remote signals or barrier semaphores. Data moves between devices by JAX's collectives and lax.ppermute only.
A program may use at most 128 MiB of HBM per device.

```python
import jax
import jax.numpy as jnp
from jax import lax

LEAF = 256
RANK = 64
RHS = 32
LEAF_DEV = 8
NEAR = 6
FAR = 6
FARC = 4
NODES = 16
LEAVES = 128
UPPER = 14
INNER = 12


def leaf_pattern(key):
    window = 3 * LEAF_DEV
    leaves = jnp.arange(LEAVES, dtype=jnp.int32)
    lowest = leaves // LEAF_DEV * LEAF_DEV - LEAF_DEV
    offsets = jnp.arange(window, dtype=jnp.int32)
    trial_cluster = lowest[:, None] + offsets[None, :]
    usable = (trial_cluster >= 0) & (trial_cluster < LEAVES) & (trial_cluster != leaves[:, None])
    scores = jax.random.randint(jax.random.fold_in(key, 11), (LEAVES, window), 0, 1 << 20, dtype=jnp.int32) * window + offsets[None, :]
    scores = jnp.where(usable, scores, (1 << 20) * window + offsets[None, :])
    ranking = jnp.argsort(scores, axis=1, stable=True)
    selected_nodes = jnp.take_along_axis(trial_cluster, ranking, axis=1)
    nearby = jnp.concatenate([leaves[:, None], selected_nodes[:, :NEAR - 1]], axis=1)
    distant = selected_nodes[:, NEAR - 1:NEAR - 1 + FAR]
    return (nearby.astype(jnp.int32), distant.astype(jnp.int32))


def draw_near_index(key, part):
    return leaf_pattern(key)[0]


def draw_leaf_list(key, part):
    return leaf_pattern(key)[1]


def draw_node_list(key, part):
    clusters = jnp.arange(NODES, dtype=jnp.int32)
    offsets = jnp.arange(1, NODES, dtype=jnp.int32)
    scores = jax.random.randint(jax.random.fold_in(key, 23), (NODES, NODES - 1), 0, 1 << 20, dtype=jnp.int32) * NODES + offsets[None, :]
    scores = jnp.where(offsets[None, :] == NODES // 2, (1 << 20) * NODES + offsets[None, :], scores)
    ranking = jnp.argsort(scores, axis=1, stable=True)
    chosen = offsets[ranking[:, :FARC - 1]]
    others = (clusters[:, None] + chosen) % NODES
    leading = (clusters + NODES // 2) % NODES
    return jnp.concatenate([leading[:, None], others], axis=1).astype(jnp.int32)


def draw_upper_list(key, part):
    nodes_here = jnp.arange(2, NODES, dtype=jnp.int32)
    level_start = jnp.ones_like(nodes_here)
    for bit_pos in range(1, 24):
        level_start = jnp.where(nodes_here >= 2 ** bit_pos, 2 ** bit_pos, level_start)
    position = nodes_here - level_start
    leading = level_start + (position + level_start // 2) % level_start
    raw_steps = jax.random.randint(jax.random.fold_in(key, 37), (UPPER, FARC - 1), 0, 1 << 20, dtype=jnp.int32)
    advance = raw_steps % jnp.maximum(level_start - 1, 1)[:, None] + 1
    others = level_start[:, None] + (position[:, None] + advance) % level_start[:, None]
    return jnp.concatenate([leading[:, None], others], axis=1).astype(jnp.int32)


def steps_of(stream_key, dims, shards, low, high):
    loudness, own = 1.0, jax.random.fold_in(stream_key, 6)
    for dim, shards_of in shards:
        draws = jnp.exp(jax.random.uniform(jax.random.fold_in(own, dim), (shards_of,), jnp.float32, low / len(shards), high / len(shards)))
        loudness = loudness * jnp.repeat(draws, dims[dim] // shards_of).reshape([-1 if axis == dim else 1 for axis in range(len(dims))])
    return loudness


def centred(stream_key, extent, deviation, most, cuts=(), kind=jnp.bfloat16):
    entries = deviation * jax.random.normal(stream_key, extent, jnp.float32)
    if cuts:
        entries = entries * steps_of(stream_key, extent, cuts, -0.22, 0.18)
    return jnp.clip(entries, -most, most).astype(kind)


def setup_inputs(seed: int = 0) -> dict:
    key_list = jax.random.split(jax.random.key(seed), 18)
    density = centred(key_list[0], (LEAVES, LEAF, RHS), 1.0, 6.0, ((0, 16), (2, 2)))
    near_blocks = centred(key_list[1], (LEAVES, NEAR, LEAF, LEAF), (LEAF * NEAR) ** -0.5, 0.15625, ((0, 16), (1, 2)))
    near_index = draw_near_index(jax.random.fold_in(key_list[17], 71), 0)
    col_basis = centred(key_list[3], (LEAVES, LEAF, RANK), LEAF ** -0.5, 0.375, ((0, 16),))
    row_basis = centred(key_list[4], (LEAVES, LEAF, RANK), RANK ** -0.5, 0.75, ((0, 16),))
    leaf_coupling = centred(key_list[5], (LEAVES, FAR, RANK, RANK), (RANK * FAR) ** -0.5, 0.3125, ((0, 16), (1, 2)))
    leaf_list = draw_leaf_list(jax.random.fold_in(key_list[17], 71), 0)
    leaf_up = centred(key_list[7], (LEAVES, RANK, RANK), (RANK * LEAF_DEV) ** -0.5, 0.25, ((0, 16),))
    leaf_down = centred(key_list[8], (LEAVES, RANK, RANK), RANK ** -0.5, 0.75, ((0, 16),))
    node_coupling = centred(key_list[9], (NODES, FARC, RANK, RANK), (RANK * FARC) ** -0.5, 0.375, ((0, 16),))
    node_list = draw_node_list(jax.random.fold_in(key_list[17], 71), 0)
    node_up = centred(key_list[11], (NODES, RANK, RANK), (2 * RANK) ** -0.5, 0.5, ((0, 16),))
    node_down = centred(key_list[12], (NODES, RANK, RANK), RANK ** -0.5, 0.75, ((0, 16),))
    upper_coupling = centred(key_list[13], (UPPER, FARC, RANK, RANK), (RANK * FARC) ** -0.5, 0.375)
    upper_list = draw_upper_list(jax.random.fold_in(key_list[17], 71), 0)
    upper_up = centred(key_list[15], (INNER, RANK, RANK), (2 * RANK) ** -0.5, 0.5)
    upper_down = centred(key_list[16], (INNER, RANK, RANK), RANK ** -0.5, 0.75)
    return dict(density=density, near_blocks=near_blocks, near_index=near_index, col_basis=col_basis, row_basis=row_basis, leaf_coupling=leaf_coupling, leaf_list=leaf_list, leaf_up=leaf_up, leaf_down=leaf_down, node_coupling=node_coupling, node_list=node_list, node_up=node_up, node_down=node_down, upper_coupling=upper_coupling, upper_list=upper_list, upper_up=upper_up, upper_down=upper_down)


def upper_tree(raised_coefficients, upper_coupling, upper_list, upper_up, upper_down, node_count):
    levels = node_count.bit_length() - 1
    rank_size = raised_coefficients.shape[1]
    columns = raised_coefficients.shape[2]
    coeffs = {}
    summed = raised_coefficients.astype(jnp.float32).reshape(node_count // 2, 2, rank_size, columns).sum(axis=1)
    coeffs[levels - 1] = summed.astype(jnp.bfloat16)
    for height in range(levels - 2, 0, -1):
        lower_size = 2 ** (height + 1)
        matrices = upper_up[lower_size - 4:2 * lower_size - 4].astype(jnp.float32)
        shifted = jnp.einsum("nrs,nrc->nsc", matrices, coeffs[height + 1].astype(jnp.float32))
        coeffs[height] = shifted.reshape(lower_size // 2, 2, rank_size, columns).sum(axis=1).astype(jnp.bfloat16)
    answer = None
    for height in range(1, levels):
        breadth = 2 ** height
        listed = upper_list[breadth - 2:2 * breadth - 2] - breadth
        sources = coeffs[height][listed]
        coupled = jnp.einsum("nfrs,nfsc->nrc", upper_coupling[breadth - 2:2 * breadth - 2].astype(jnp.float32), sources.astype(jnp.float32))
        if height > 1:
            parents = jnp.repeat(answer, 2, axis=0)
            coupled = coupled + jnp.einsum("nrs,nsc->nrc", upper_down[breadth - 4:2 * breadth - 4].astype(jnp.float32), parents.astype(jnp.float32))
        answer = coupled.astype(jnp.bfloat16)
    return answer


def reference(density, near_blocks, near_index, col_basis, row_basis, leaf_coupling, leaf_list, leaf_up, leaf_down, node_coupling, node_list, node_up, node_down, upper_coupling, upper_list, upper_up, upper_down):
    leaf_coeff = jnp.einsum("tlr,tlc->trc", col_basis.astype(jnp.float32), density.astype(jnp.float32)).astype(jnp.bfloat16)
    far_sources = leaf_coeff[leaf_list]
    far_field = jnp.einsum("tjrs,tjsc->trc", leaf_coupling.astype(jnp.float32), far_sources.astype(jnp.float32))
    grouped_up = leaf_up.reshape(NODES, LEAF_DEV, RANK, RANK).astype(jnp.float32)
    grouped_coeff = leaf_coeff.reshape(NODES, LEAF_DEV, RANK, RHS).astype(jnp.float32)
    node_coeff = jnp.einsum("ntrs,ntrc->nsc", grouped_up, grouped_coeff).astype(jnp.bfloat16)
    raised_coefficients = jnp.einsum("nrs,nrc->nsc", node_up.astype(jnp.float32), node_coeff.astype(jnp.float32)).astype(jnp.bfloat16)
    answer = upper_tree(raised_coefficients, upper_coupling, upper_list, upper_up, upper_down, NODES)
    node_term = jnp.einsum("nfrs,nfsc->nrc", node_coupling.astype(jnp.float32), node_coeff[node_list].astype(jnp.float32))
    parents = jnp.repeat(answer, 2, axis=0)
    node_term = node_term + jnp.einsum("nrs,nsc->nrc", node_down.astype(jnp.float32), parents.astype(jnp.float32))
    node_field = node_term.astype(jnp.bfloat16)
    grouped_down = leaf_down.reshape(NODES, LEAF_DEV, RANK, RANK).astype(jnp.float32)
    descended = jnp.einsum("ntrs,nsc->ntrc", grouped_down, node_field.astype(jnp.float32)).reshape(LEAVES, RANK, RHS)
    leaf_field = (far_field + descended).astype(jnp.bfloat16)

    def device_near(block_number):
        row_start = block_number * LEAF_DEV
        block_entries = lax.dynamic_slice_in_dim(near_blocks, row_start, LEAF_DEV, 0)
        indices = lax.dynamic_slice_in_dim(near_index, row_start, LEAF_DEV, 0)
        selected_nodes = density[indices]
        return jnp.einsum("vpqx,vpxn->vqn", block_entries.astype(jnp.float32), selected_nodes.astype(jnp.float32))

    proximate_field = lax.map(device_near, jnp.arange(NODES, dtype=jnp.int32)).reshape(LEAVES, LEAF, RHS)
    farther = jnp.einsum("tlr,trc->tlc", row_basis.astype(jnp.float32), leaf_field.astype(jnp.float32))
    return (proximate_field + farther).astype(jnp.bfloat16)
```

```python
import jax
import jax.numpy as jnp
from jax import lax
from jax.experimental import pallas as pl
from jax.experimental.pallas import tpu as pltpu
from jax.sharding import PartitionSpec as P

LAST = (((1,), (1,)), ((), ()))
PLAIN = (((1,), (0,)), ((), ()))


def mm(a, b, dims):
    return lax.dot_general(a, b, dims, preferred_element_type=jnp.float32)


def vmem():
    return pl.BlockSpec(memory_space=pltpu.VMEM)


def smem():
    return pl.BlockSpec(memory_space=pltpu.SMEM)


def anywhere():
    return pl.BlockSpec(memory_space=pl.ANY)


def up_kernel(dens, col, leaf_up, node_up, pack, message):
    leaves, _, points = dens.shape
    rank = col.shape[1]
    halves = points // 128
    node = None
    for t in range(leaves):
        here = dens[t]
        for h in range(halves):
            pack[t * halves + h] = here[:, h * 128 : (h + 1) * 128]
        coeff = mm(here, col[t], LAST).astype(jnp.bfloat16)
        side = t % 2
        pack[leaves * halves + t // 2, :, side * rank : (side + 1) * rank] = coeff
        term = mm(coeff, leaf_up[t], PLAIN)
        node = term if node is None else node + term
    node = node.astype(jnp.bfloat16)
    message[:, :rank] = node
    message[:, rank:] = mm(node, node_up[0], PLAIN).astype(jnp.bfloat16)


def field_kernel(
    lists, lists_other, low, own, high, near, near_other, coup, coup_other,
    near_out, far_out, ext, ext_coeff, blocks, sems,
):
    leaves, entries = near.shape[0], near.shape[1]
    rank = coup.shape[-1]
    points = near.shape[-1]
    halves = points // 128
    copies = []
    for t in range(leaves):
        pair = []
        for s, ref in enumerate((near, near_other)):
            copy = pltpu.make_async_copy(
                ref.at[t], blocks.at[t, pl.ds(s * entries, entries)], sems.at[t, s]
            )
            copy.start()
            pair.append(copy)
        copies.append(pair)
    for b, ref in enumerate((low, own, high)):
        for t in range(leaves):
            for h in range(halves):
                ext[b * leaves + t, :, h * 128 : (h + 1) * 128] = ref[t * halves + h]
            side = t % 2
            ext_coeff[b * leaves + t] = ref[
                leaves * halves + t // 2, :, side * rank : (side + 1) * rank
            ]
    offset = (lax.axis_index("leaf") - 1) * leaves
    for t in range(leaves):
        total = None
        for s, table in enumerate((lists, lists_other)):
            for j in range(entries):
                source = ext_coeff[table[entries + j, t] - offset]
                matrix = (coup, coup_other)[s][t, j]
                term = mm(source, matrix, LAST)
                total = term if total is None else total + term
        far_out[t] = total
    for t in range(leaves):
        for copy in copies[t]:
            copy.wait()
        total = None
        for s, table in enumerate((lists, lists_other)):
            for j in range(entries):
                source = ext[table[j, t] - offset]
                term = mm(source, blocks[t, s * entries + j], LAST)
                total = term if total is None else total + term
        near_out[t] = total


def down_kernel(
    node_list, upper_list, gathered, near, far, row, leaf_down, node_coup, node_down,
    upper_coup, upper_up, upper_down, out, *tree,
):
    nodes, columns, _ = gathered.shape
    rank = row.shape[1]
    leaves = row.shape[0]
    farc = node_coup.shape[1]
    levels = nodes.bit_length() - 1
    me = lax.axis_index("leaf")

    for m in range(nodes // 2):
        left = gathered[(2 * m) ^ me, :, rank:].astype(jnp.float32)
        right = gathered[(2 * m + 1) ^ me, :, rank:].astype(jnp.float32)
        tree[levels - 2][m] = (left + right).astype(jnp.bfloat16)
    for height in range(levels - 2, 0, -1):
        breadth = 2**height
        lower = tree[height]
        for m in range(breadth):
            first = 2 * (breadth + m) - 4
            value = mm(lower[2 * m], upper_up[first], PLAIN)
            value = value + mm(lower[2 * m + 1], upper_up[first + 1], PLAIN)
            tree[height - 1][m] = value.astype(jnp.bfloat16)
    field = None
    for height in range(1, levels):
        breadth = 2**height
        node = (nodes + me) >> (levels - height)
        total = None
        for j in range(farc):
            source = tree[height - 1][upper_list[j, node - 2] - breadth]
            term = mm(source, upper_coup[node - 2, j], LAST)
            total = term if total is None else total + term
        if height > 1:
            total = total + mm(field, upper_down[node - 4], LAST)
        field = total.astype(jnp.bfloat16)
    total = mm(field, node_down[0], LAST)
    for j in range(farc):
        source = gathered[node_list[0, j] ^ me, :, :rank]
        total = total + mm(source, node_coup[0, j], LAST)
    field = total.astype(jnp.bfloat16)
    for t in range(leaves):
        local = (far[t] + mm(field, leaf_down[t], LAST)).astype(jnp.bfloat16)
        out[t] = (near[t] + mm(local, row[t], PLAIN)).astype(jnp.bfloat16)


def body(
    density,
    near_blocks,
    near_index,
    col_basis,
    row_basis,
    leaf_coupling,
    leaf_list,
    leaf_up,
    leaf_down,
    node_coupling,
    node_list,
    node_up,
    node_down,
    upper_coupling,
    upper_list,
    upper_up,
    upper_down,
):
    leaves, points, columns = density.shape
    rank = col_basis.shape[2]
    nodes = lax.axis_size("leaf")
    levels = nodes.bit_length() - 1
    bf16, f32 = jnp.bfloat16, jnp.float32
    swap = [(0, 1), (1, 0)]

    near_other = lax.ppermute(near_blocks, "sub", swap)
    coup_other = lax.ppermute(leaf_coupling, "sub", swap)
    lists = jnp.concatenate([near_index.T, leaf_list.T], axis=0)
    lists_other = lax.ppermute(lists, "sub", swap)

    dens = jnp.swapaxes(density, 1, 2)
    tiles = leaves * (points // 128) + leaves // 2
    pack, message = pl.pallas_call(
        up_kernel,
        out_shape=(
            jax.ShapeDtypeStruct((tiles, columns, 128), bf16),
            jax.ShapeDtypeStruct((columns, 2 * rank), bf16),
        ),
        in_specs=[vmem()] * 4,
        out_specs=(vmem(), vmem()),
        name="up",
    )(dens, jnp.swapaxes(col_basis, 1, 2), leaf_up, node_up)

    low = lax.ppermute(pack, "leaf", [(i, i + 1) for i in range(nodes - 1)])
    high = lax.ppermute(pack, "leaf", [(i + 1, i) for i in range(nodes - 1)])
    gathered = message[None]
    for bit in range(levels):
        step = 1 << bit
        other = lax.ppermute(gathered, "leaf", [(i, i ^ step) for i in range(nodes)])
        gathered = jnp.concatenate([gathered, other], axis=0)

    entries = near_blocks.shape[1]
    near, far = pl.pallas_call(
        field_kernel,
        out_shape=(
            jax.ShapeDtypeStruct((leaves, columns, points), f32),
            jax.ShapeDtypeStruct((leaves, columns, rank), f32),
        ),
        in_specs=[smem()] * 2 + [vmem()] * 3 + [anywhere()] * 2 + [vmem()] * 2,
        out_specs=(vmem(), vmem()),
        scratch_shapes=[
            pltpu.VMEM((3 * leaves, columns, points), bf16),
            pltpu.VMEM((3 * leaves, columns, rank), bf16),
            pltpu.VMEM((leaves, 2 * entries, points, points), bf16),
            pltpu.SemaphoreType.DMA((leaves, 2)),
        ],
        compiler_params=pltpu.CompilerParams(vmem_limit_bytes=24 * 1024 * 1024),
        cost_estimate=pl.CostEstimate(
            flops=2 * leaves * 2 * entries * points * points * 128,
            bytes_accessed=leaves * 2 * entries * points * points * 2,
            transcendentals=0,
        ),
        name="field",
    )(lists, lists_other, low, pack, high, near_blocks, near_other, leaf_coupling, coup_other)

    out = pl.pallas_call(
        down_kernel,
        out_shape=jax.ShapeDtypeStruct((leaves, columns, points), bf16),
        in_specs=[smem()] * 2 + [vmem()] * 10,
        out_specs=vmem(),
        scratch_shapes=[
            pltpu.VMEM((2**height, columns, rank), bf16) for height in range(1, levels)
        ],
        compiler_params=pltpu.CompilerParams(vmem_limit_bytes=24 * 1024 * 1024),
        name="down",
    )(
        node_list, upper_list.T, gathered, near, far, jnp.swapaxes(row_basis, 1, 2), leaf_down,
        node_coupling, node_down, upper_coupling, upper_up, upper_down,
    )
    return jnp.swapaxes(out, 1, 2)


def solution(mesh):
    placed = (
        P("leaf", None, "sub"),
        P("leaf", "sub", None, None),
        P("leaf", "sub"),
        P("leaf", None, None),
        P("leaf", None, None),
        P("leaf", "sub", None, None),
        P("leaf", "sub"),
        P("leaf", None, None),
        P("leaf", None, None),
        P("leaf", None, None, None),
        P("leaf", None),
        P("leaf", None, None),
        P("leaf", None, None),
        P(),
        P(),
        P(),
        P(),
    )
    return jax.shard_map(
        body, mesh=mesh, in_specs=placed, out_specs=P("leaf", None, "sub"), check_vma=False
    )
```

```python
import functools

import jax
import jax.numpy as jnp
from jax import lax
from jax.experimental import pallas as pl
from jax.experimental.pallas import tpu as pltpu
from jax.sharding import PartitionSpec as P

LAST = (((1,), (1,)), ((), ()))
PLAIN = (((1,), (0,)), ((), ()))


def mm(a, b, dims):
    return lax.dot_general(a, b, dims, preferred_element_type=jnp.float32)


def vmem():
    return pl.BlockSpec(memory_space=pltpu.VMEM)


def smem():
    return pl.BlockSpec(memory_space=pltpu.SMEM)


def anywhere():
    return pl.BlockSpec(memory_space=pl.ANY)


def up_kernel(dens, col, leaf_up, node_up, coeff_out, message):
    leaves = dens.shape[0]
    rank = col.shape[1]
    node = None
    for t in range(leaves):
        coeff = mm(dens[t], col[t], LAST).astype(jnp.bfloat16)
        coeff_out[t] = coeff
        term = mm(coeff, leaf_up[t], PLAIN)
        node = term if node is None else node + term
    node = node.astype(jnp.bfloat16)
    message[:, :rank] = node
    message[:, rank:] = mm(node, node_up[0], PLAIN).astype(jnp.bfloat16)


def pack_kernel(dens, coeff, near, _, __, pack, near_out, sem):
    copy = pltpu.make_async_copy(near, near_out, sem)
    copy.start()
    leaves, _, points = dens.shape
    rank = coeff.shape[2]
    halves = points // 128
    for t in range(leaves):
        here = dens[t]
        for h in range(halves):
            pack[t * halves + h] = here[:, h * 128 : (h + 1) * 128]
        side = t % 2
        pack[leaves * halves + t // 2, :, side * rank : (side + 1) * rank] = coeff[t]
    copy.wait()


def field_kernel(
    first, lists, lists_other, pair, own, cross, near, near_other, coup, coup_other, _,
    near_out, far_out, ext, ext_coeff,
):
    leaves, entries = near.shape[0], near.shape[1]
    count = near_out.shape[0]
    rank = coup.shape[-1]
    points = near.shape[-1]
    halves = points // 128
    me = lax.axis_index("leaf")
    odd = me & 1
    for slot, ref in ((2 - 2 * odd, pair), (1, own), (2 * odd, cross)):
        for t in range(leaves):
            for h in range(halves):
                ext[slot * leaves + t, :, h * 128 : (h + 1) * 128] = ref[t * halves + h]
            side = t % 2
            ext_coeff[slot * leaves + t] = ref[
                leaves * halves + t // 2, :, side * rank : (side + 1) * rank
            ]
    offset = (me - 1) * leaves
    for k in range(count):
        t = first + k
        total = None
        for table, matrices in ((lists, coup), (lists_other, coup_other)):
            for j in range(entries):
                source = ext_coeff[table[entries + j, t] - offset]
                term = mm(source, matrices[t, j], LAST)
                total = term if total is None else total + term
        far_out[k] = total
        total = None
        for table, blocks in ((lists, near), (lists_other, near_other)):
            for j in range(entries):
                term = mm(ext[table[j, t] - offset], blocks[t, j], LAST)
                total = term if total is None else total + term
        near_out[k] = total


def down_kernel(
    node_list, upper_list, known, other, near, near_late, far, far_late, row, leaf_down, node_coup, node_down,
    upper_coup, upper_up, upper_down, out, *tree,
):
    half_nodes, columns, _ = known.shape
    nodes = 2 * half_nodes
    rank = row.shape[1]
    leaves = row.shape[0]
    gathered, tree = tree[0], tree[1:]
    gathered[:half_nodes] = known[...]
    gathered[half_nodes:] = other[...]
    farc = node_coup.shape[1]
    levels = nodes.bit_length() - 1
    me = lax.axis_index("leaf")

    for m in range(nodes // 2):
        left = gathered[(2 * m) ^ me, :, rank:].astype(jnp.float32)
        right = gathered[(2 * m + 1) ^ me, :, rank:].astype(jnp.float32)
        tree[levels - 2][m] = (left + right).astype(jnp.bfloat16)
    for height in range(levels - 2, 0, -1):
        breadth = 2**height
        lower = tree[height]
        for m in range(breadth):
            first = 2 * (breadth + m) - 4
            value = mm(lower[2 * m], upper_up[first], PLAIN)
            value = value + mm(lower[2 * m + 1], upper_up[first + 1], PLAIN)
            tree[height - 1][m] = value.astype(jnp.bfloat16)
    field = None
    for height in range(1, levels):
        breadth = 2**height
        node = (nodes + me) >> (levels - height)
        total = None
        for j in range(farc):
            source = tree[height - 1][upper_list[j, node - 2] - breadth]
            term = mm(source, upper_coup[node - 2, j], LAST)
            total = term if total is None else total + term
        if height > 1:
            total = total + mm(field, upper_down[node - 4], LAST)
        field = total.astype(jnp.bfloat16)
    total = mm(field, node_down[0], LAST)
    for j in range(farc):
        source = gathered[node_list[0, j] ^ me, :, :rank]
        total = total + mm(source, node_coup[0, j], LAST)
    field = total.astype(jnp.bfloat16)
    half = near.shape[0]
    for t in range(leaves):
        near_here, far_here = (near[t], far[t]) if t < half else (near_late[t - half], far_late[t - half])
        local = (far_here + mm(field, leaf_down[t], LAST)).astype(jnp.bfloat16)
        out[t] = (near_here + mm(local, row[t], PLAIN)).astype(jnp.bfloat16)


def body(
    density,
    near_blocks,
    near_index,
    col_basis,
    row_basis,
    leaf_coupling,
    leaf_list,
    leaf_up,
    leaf_down,
    node_coupling,
    node_list,
    node_up,
    node_down,
    upper_coupling,
    upper_list,
    upper_up,
    upper_down,
):
    leaves, points, columns = density.shape
    rank = col_basis.shape[2]
    nodes = lax.axis_size("leaf")
    levels = nodes.bit_length() - 1
    bf16, f32 = jnp.bfloat16, jnp.float32
    swap = [(0, 1), (1, 0)]

    near_other = lax.ppermute(near_blocks, "sub", swap)
    coup_other = lax.ppermute(leaf_coupling, "sub", swap)
    lists = jnp.concatenate([near_index.T, leaf_list.T], axis=0)
    lists_other = lax.ppermute(lists, "sub", swap)

    dens = jnp.swapaxes(density, 1, 2)
    coeff, message = pl.pallas_call(
        up_kernel,
        out_shape=(
            pltpu.VMEM((leaves, columns, rank), bf16),
            pltpu.VMEM((columns, 2 * rank), bf16),
        ),
        in_specs=[vmem()] * 4,
        out_specs=(vmem(), vmem()),
        name="up",
    )(dens, jnp.swapaxes(col_basis, 1, 2), leaf_up, node_up)
    tiles = leaves * (points // 128) + leaves // 2
    pack, near_here = pl.pallas_call(
        pack_kernel,
        out_shape=(
            pltpu.VMEM((tiles, columns, 128), bf16),
            pltpu.VMEM(near_blocks.shape, bf16),
        ),
        in_specs=[vmem()] * 2 + [anywhere()] * 3,
        out_specs=(vmem(), vmem()),
        scratch_shapes=[pltpu.SemaphoreType.DMA],
        name="pack",
    )(
        dens, coeff, pltpu.with_memory_space_constraint(near_blocks, pltpu.HBM), coup_other,
        lists_other,
    )
    inner = [(i, (i + 1 if i % 2 else i - 1)) for i in range(1, nodes - 1)]
    pair = lax.ppermute(pack, "leaf", [(i, i ^ 1) for i in range(nodes)])
    cross = lax.ppermute(pack, "leaf", inner + [(0, 0), (nodes - 1, nodes - 1)])

    entries = near_blocks.shape[1]
    half = leaves // 2

    def fields(first, after):
        return pl.pallas_call(
            functools.partial(field_kernel, first),
            out_shape=(
                jax.ShapeDtypeStruct((half, columns, points), f32),
                jax.ShapeDtypeStruct((half, columns, rank), f32),
            ),
            in_specs=[smem()] * 2 + [vmem()] * 7 + [anywhere()],
            out_specs=(vmem(), vmem()),
            scratch_shapes=[
                pltpu.VMEM((3 * leaves, columns, points), bf16),
                pltpu.VMEM((3 * leaves, columns, rank), bf16),
            ],
            compiler_params=pltpu.CompilerParams(vmem_limit_bytes=24 * 1024 * 1024),
            cost_estimate=pl.CostEstimate(
                flops=2 * half * 2 * entries * points * points * 256,
                bytes_accessed=half * 2 * entries * points * points * 2,
                transcendentals=0,
            ),
            name="fields",
        )(
            lists, lists_other, pair, pack, cross, near_here, near_other, leaf_coupling,
            coup_other, after,
        )

    known = message[None]
    near = far = near_late = far_late = None
    for bit in range(levels):
        step = 1 << bit
        other = lax.ppermute(known, "leaf", [(i, i ^ step) for i in range(nodes)])
        if bit == 0:
            known, other, pack = lax.optimization_barrier((known, other, pack))
        if bit == levels - 2:
            near, far = fields(0, known)
            known, other, near, far = lax.optimization_barrier((known, other, near, far))
        if bit == levels - 1:
            near_late, far_late = fields(half, known)
        else:
            known = jnp.concatenate([known, other], axis=0)

    out = pl.pallas_call(
        down_kernel,
        out_shape=jax.ShapeDtypeStruct((leaves, columns, points), bf16),
        in_specs=[smem()] * 2 + [vmem()] * 13,
        out_specs=vmem(),
        scratch_shapes=[pltpu.VMEM((nodes, columns, 2 * rank), bf16)]
        + [pltpu.VMEM((2**height, columns, rank), bf16) for height in range(1, levels)],
        compiler_params=pltpu.CompilerParams(vmem_limit_bytes=24 * 1024 * 1024),
        name="down",
    )(
        node_list, upper_list.T, known, other, near, near_late, far, far_late,
        jnp.swapaxes(row_basis, 1, 2), leaf_down, node_coupling, node_down, upper_coupling, upper_up, upper_down,
    )
    return jnp.swapaxes(out, 1, 2)


def solution(mesh):
    placed = (
        P("leaf", None, "sub"),
        P("leaf", "sub", None, None),
        P("leaf", "sub"),
        P("leaf", None, None),
        P("leaf", None, None),
        P("leaf", "sub", None, None),
        P("leaf", "sub"),
        P("leaf", None, None),
        P("leaf", None, None),
        P("leaf", None, None, None),
        P("leaf", None),
        P("leaf", None, None),
        P("leaf", None, None),
        P(),
        P(),
        P(),
        P(),
    )
    return jax.shard_map(
        body, mesh=mesh, in_specs=placed, out_specs=P("leaf", None, "sub"), check_vma=False
    )
```

```python
import functools

import jax
import jax.numpy as jnp
from jax import lax
from jax.experimental import pallas as pl
from jax.experimental.pallas import tpu as pltpu
from jax.sharding import PartitionSpec as P

LAST = (((1,), (1,)), ((), ()))
PLAIN = (((1,), (0,)), ((), ()))


def mm(a, b, dims):
    return lax.dot_general(a, b, dims, preferred_element_type=jnp.float32)


def pinned(x, space):
    return pltpu.with_memory_space_constraint(x, space)


def vmem():
    return pl.BlockSpec(memory_space=pltpu.VMEM)


def smem():
    return pl.BlockSpec(memory_space=pltpu.SMEM)


def anywhere():
    return pl.BlockSpec(memory_space=pl.ANY)


def up_kernel(dens, col, leaf_up, node_up, coeff_out, message):
    leaves = dens.shape[0]
    rank = col.shape[1]
    node = None
    for t in range(leaves):
        coeff = mm(dens[t], col[t], LAST).astype(jnp.bfloat16)
        coeff_out[t] = coeff
        term = mm(coeff, leaf_up[t], PLAIN)
        node = term if node is None else node + term
    node = node.astype(jnp.bfloat16)
    message[:, :rank] = node
    message[:, rank:] = mm(node, node_up[0], PLAIN).astype(jnp.bfloat16)


def pack_kernel(dens, coeff, coup, near_list, far_list, pack, *rest):
    copies = [
        pltpu.make_async_copy(source, target, rest[3].at[k])
        for k, (source, target) in enumerate(zip((coup, near_list, far_list), rest[:3]))
    ]
    for copy in copies:
        copy.start()
    leaves, _, points = dens.shape
    rank = coeff.shape[2]
    halves = points // 128
    for t in range(leaves):
        here = dens[t]
        for h in range(halves):
            pack[t * halves + h] = here[:, h * 128 : (h + 1) * 128]
        side = t % 2
        pack[leaves * halves + t // 2, :, side * rank : (side + 1) * rank] = coeff[t]
    for copy in copies:
        copy.wait()


def field_kernel(
    first, near_list, far_list, near_list_other, far_list_other, pair, own, cross,
    coup, coup_other, near, near_other, near_out, far_out, ext, ext_coeff, blocks, sems,
):
    leaves, entries = near.shape[0], near.shape[1]
    count = near_out.shape[0]
    rank = coup.shape[-1]
    points = near.shape[-1]
    halves = points // 128
    copies = []
    for k in range(count):
        copy = pltpu.make_async_copy(near.at[first + k], blocks.at[k], sems.at[k])
        copy.start()
        copies.append(copy)
    me = lax.axis_index("leaf")
    odd = me & 1
    for slot, ref in ((2 - 2 * odd, pair), (1, own), (2 * odd, cross)):
        for t in range(leaves):
            for h in range(halves):
                ext[slot * leaves + t, :, h * 128 : (h + 1) * 128] = ref[t * halves + h]
            side = t % 2
            ext_coeff[slot * leaves + t] = ref[
                leaves * halves + t // 2, :, side * rank : (side + 1) * rank
            ]
    offset = (me - 1) * leaves
    for k in range(count):
        total = None
        for table, matrices in ((far_list, coup), (far_list_other, coup_other)):
            for j in range(entries):
                source = ext_coeff[table[j, first + k] - offset]
                term = mm(source, matrices[first + k, j], LAST)
                total = term if total is None else total + term
        far_out[k] = total
    for k in range(count):
        total = None
        for j in range(entries):
            source = ext[near_list_other[j, first + k] - offset]
            term = mm(source, near_other[first + k, j], LAST)
            total = term if total is None else total + term
        near_out[k] = total
    for k in range(count):
        copies[k].wait()
        total = near_out[k]
        for j in range(entries):
            source = ext[near_list[j, first + k] - offset]
            total = total + mm(source, blocks[k, j], LAST)
        near_out[k] = total


def down_kernel(
    node_list, upper_list, known, other, near, near_late, far, far_late, row, leaf_down, node_coup, node_down,
    upper_coup, upper_up, upper_down, out, *tree,
):
    half_nodes, columns, _ = known.shape
    nodes = 2 * half_nodes
    rank = row.shape[1]
    leaves = row.shape[0]
    gathered, tree = tree[0], tree[1:]
    gathered[:half_nodes] = known[...]
    gathered[half_nodes:] = other[...]
    farc = node_coup.shape[1]
    levels = nodes.bit_length() - 1
    me = lax.axis_index("leaf")

    for m in range(nodes // 2):
        left = gathered[(2 * m) ^ me, :, rank:].astype(jnp.float32)
        right = gathered[(2 * m + 1) ^ me, :, rank:].astype(jnp.float32)
        tree[levels - 2][m] = (left + right).astype(jnp.bfloat16)
    for height in range(levels - 2, 0, -1):
        breadth = 2**height
        lower = tree[height]
        for m in range(breadth):
            first = 2 * (breadth + m) - 4
            value = mm(lower[2 * m], upper_up[first], PLAIN)
            value = value + mm(lower[2 * m + 1], upper_up[first + 1], PLAIN)
            tree[height - 1][m] = value.astype(jnp.bfloat16)
    field = None
    for height in range(1, levels):
        breadth = 2**height
        node = (nodes + me) >> (levels - height)
        total = None
        for j in range(farc):
            source = tree[height - 1][upper_list[j, node - 2] - breadth]
            term = mm(source, upper_coup[node - 2, j], LAST)
            total = term if total is None else total + term
        if height > 1:
            total = total + mm(field, upper_down[node - 4], LAST)
        field = total.astype(jnp.bfloat16)
    total = mm(field, node_down[0], LAST)
    for j in range(farc):
        source = gathered[node_list[0, j] ^ me, :, :rank]
        total = total + mm(source, node_coup[0, j], LAST)
    field = total.astype(jnp.bfloat16)
    half = near.shape[0]
    for t in range(leaves):
        near_here, far_here = (near[t], far[t]) if t < half else (near_late[t - half], far_late[t - half])
        local = (far_here + mm(field, leaf_down[t], LAST)).astype(jnp.bfloat16)
        out[t] = (near_here + mm(local, row[t], PLAIN)).astype(jnp.bfloat16)


def body(
    density,
    near_blocks,
    near_index,
    col_basis,
    row_basis,
    leaf_coupling,
    leaf_list,
    leaf_up,
    leaf_down,
    node_coupling,
    node_list,
    node_up,
    node_down,
    upper_coupling,
    upper_list,
    upper_up,
    upper_down,
):
    leaves, points, columns = density.shape
    rank = col_basis.shape[2]
    nodes = lax.axis_size("leaf")
    levels = nodes.bit_length() - 1
    bf16, f32 = jnp.bfloat16, jnp.float32
    swap = [(0, 1), (1, 0)]

    near_other = lax.ppermute(near_blocks, "sub", swap)
    coup_other = lax.ppermute(leaf_coupling, "sub", swap)
    near_list, far_list = near_index.T, leaf_list.T
    near_list_other = lax.ppermute(near_list, "sub", swap)
    far_list_other = lax.ppermute(far_list, "sub", swap)

    dens = jnp.swapaxes(density, 1, 2)
    coeff, message = pl.pallas_call(
        up_kernel,
        out_shape=(
            pltpu.VMEM((leaves, columns, rank), bf16),
            pltpu.VMEM((columns, 2 * rank), bf16),
        ),
        in_specs=[vmem()] * 4,
        out_specs=(vmem(), vmem()),
        name="up",
    )(dens, jnp.swapaxes(col_basis, 1, 2), leaf_up, node_up)
    tiles = leaves * (points // 128) + leaves // 2
    hbm, fast = pltpu.HBM, pltpu.VMEM
    pack, coup_here, near_list, far_list = pl.pallas_call(
        pack_kernel,
        out_shape=(
            pltpu.VMEM((tiles, columns, 128), bf16),
            pltpu.VMEM(leaf_coupling.shape, bf16),
            pltpu.VMEM(near_list.shape, near_list.dtype),
            pltpu.VMEM(far_list.shape, far_list.dtype),
        ),
        in_specs=[vmem()] * 2 + [anywhere()] * 3,
        out_specs=(vmem(),) * 4,
        scratch_shapes=[pltpu.SemaphoreType.DMA((3,))],
        name="pack",
    )(
        pinned(dens, hbm), pinned(coeff, fast), pinned(leaf_coupling, hbm),
        pinned(near_list, hbm), pinned(far_list, hbm),
    )
    pair = lax.ppermute(pack, "leaf", [(i, i ^ 1) for i in range(nodes)])
    others = [(i, (i + 1 if i % 2 else i - 1) % nodes) for i in range(nodes)]

    entries = near_blocks.shape[1]
    half = leaves // 2

    def fields(first):
        operands = [near_list, far_list, near_list_other, far_list_other]
        operands += [pair, pack, cross, coup_here, coup_other]
        operands = [pinned(x, fast) for x in operands]
        operands += [pinned(near_blocks, hbm), pinned(near_other, fast)]
        return pl.pallas_call(
            functools.partial(field_kernel, first),
            out_shape=(
                pltpu.VMEM((half, columns, points), f32),
                pltpu.VMEM((half, columns, rank), f32),
            ),
            in_specs=[smem()] * 4 + [vmem()] * 5 + [anywhere(), vmem()],
            out_specs=(vmem(), vmem()),
            scratch_shapes=[
                pltpu.VMEM((3 * leaves, columns, points), bf16),
                pltpu.VMEM((3 * leaves, columns, rank), bf16),
                pltpu.VMEM((half, entries, points, points), bf16),
                pltpu.SemaphoreType.DMA((half,)),
            ],
            compiler_params=pltpu.CompilerParams(vmem_limit_bytes=16 * 1024 * 1024),
            cost_estimate=pl.CostEstimate(
                flops=2 * half * 2 * entries * points * points * 256,
                bytes_accessed=half * 2 * entries * points * points * 2,
                transcendentals=0,
            ),
            name="fields",
        )(*operands)

    known = message[None]
    for bit in range(levels):
        step = 1 << bit
        other = lax.ppermute(known, "leaf", [(i, i ^ step) for i in range(nodes)])
        if bit == 0:
            known, other, pack = lax.optimization_barrier((known, other, pack))
            cross = lax.ppermute(pack, "leaf", others)
        if bit == 1:
            known, other, coup_other, near_list_other, far_list_other = lax.optimization_barrier(
                (known, other, coup_other, near_list_other, far_list_other)
            )
        if bit == levels - 2:
            known, cross = lax.optimization_barrier((known, cross))
            near, far = fields(0)
            known, other, near, far = lax.optimization_barrier((known, other, near, far))
        if bit == levels - 1:
            known, cross = lax.optimization_barrier((known, cross))
            near_late, far_late = fields(half)
        else:
            known = jnp.concatenate([known, other], axis=0)

    out = pl.pallas_call(
        down_kernel,
        out_shape=jax.ShapeDtypeStruct((leaves, columns, points), bf16),
        in_specs=[smem()] * 2 + [vmem()] * 13,
        out_specs=vmem(),
        scratch_shapes=[pltpu.VMEM((nodes, columns, 2 * rank), bf16)]
        + [pltpu.VMEM((2**height, columns, rank), bf16) for height in range(1, levels)],
        compiler_params=pltpu.CompilerParams(vmem_limit_bytes=24 * 1024 * 1024),
        name="down",
    )(
        node_list, upper_list.T, known, other, near, near_late, far, far_late,
        jnp.swapaxes(row_basis, 1, 2), leaf_down, node_coupling, node_down, upper_coupling, upper_up, upper_down,
    )
    return jnp.swapaxes(out, 1, 2)


def solution(mesh):
    placed = (
        P("leaf", None, "sub"),
        P("leaf", "sub", None, None),
        P("leaf", "sub"),
        P("leaf", None, None),
        P("leaf", None, None),
        P("leaf", "sub", None, None),
        P("leaf", "sub"),
        P("leaf", None, None),
        P("leaf", None, None),
        P("leaf", None, None, None),
        P("leaf", None),
        P("leaf", None, None),
        P("leaf", None, None),
        P(),
        P(),
        P(),
        P(),
    )
    return jax.shard_map(
        body, mesh=mesh, in_specs=placed, out_specs=P("leaf", None, "sub"), check_vma=False
    )
```

```python
import jax
import jax.numpy as jnp
from jax import lax
from jax.experimental import pallas as pl
from jax.experimental.pallas import tpu as pltpu
from jax.sharding import PartitionSpec as P

LAST = (((1,), (1,)), ((), ()))
PLAIN = (((1,), (0,)), ((), ()))


def mm(a, b, dims):
    return lax.dot_general(a, b, dims, preferred_element_type=jnp.float32)


def vmem():
    return pl.BlockSpec(memory_space=pltpu.VMEM)


def smem():
    return pl.BlockSpec(memory_space=pltpu.SMEM)


def up_kernel(dens, col, leaf_up, node_up, coeff_out, message):
    leaves = dens.shape[0]
    rank = col.shape[1]
    node = None
    for t in range(leaves):
        coeff = mm(dens[t], col[t], LAST).astype(jnp.bfloat16)
        coeff_out[t] = coeff
        term = mm(coeff, leaf_up[t], PLAIN)
        node = term if node is None else node + term
    node = node.astype(jnp.bfloat16)
    message[:, :rank] = node
    message[:, rank:] = mm(node, node_up[0], PLAIN).astype(jnp.bfloat16)


def pack_rows(pack, t, leaves, long, short):
    halves = long.shape[1] // 128
    rank = short.shape[1]
    for h in range(halves):
        pack[t * halves + h] = long[:, h * 128 : (h + 1) * 128]
    side = t % 2
    pack[leaves * halves + t // 2, :, side * rank : (side + 1) * rank] = short


def unpack_long(pack, t, halves):
    return jnp.concatenate([pack[t * halves + h] for h in range(halves)], axis=1)


def unpack_short(pack, t, leaves, halves, rank):
    side = t % 2
    return pack[leaves * halves + t // 2, :, side * rank : (side + 1) * rank]


def pack_kernel(dens, coeff, pack):
    leaves = dens.shape[0]
    for t in range(leaves):
        pack_rows(pack, t, leaves, dens[t], coeff[t])


def stage_kernel(*refs):
    count = len(refs) // 2
    sems = refs[-1]
    copies = [
        pltpu.make_async_copy(source, target, sems.at[k])
        for k, (source, target) in enumerate(zip(refs[:count], refs[count:-1]))
    ]
    for copy in copies:
        copy.start()
    for copy in copies:
        copy.wait()


def field_kernel(
    near_list, far_list, pair, own, cross, pair_other, own_other, cross_other, coup, near,
    near_out, far_out, send, ext, ext_coeff,
):
    leaves, entries = near.shape[0], near.shape[1]
    columns = own.shape[1]
    rank = coup.shape[-1]
    halves = near.shape[-1] // 128
    me = lax.axis_index("leaf")
    odd = me & 1
    for slot, pair_of_cores in (
        (2 - 2 * odd, (pair, pair_other)),
        (1, (own, own_other)),
        (2 * odd, (cross, cross_other)),
    ):
        for c, ref in enumerate(pair_of_cores):
            rows = slice(c * columns, (c + 1) * columns)
            for t in range(leaves):
                ext[slot * leaves + t, rows] = unpack_long(ref, t, halves)
                ext_coeff[slot * leaves + t, rows] = unpack_short(ref, t, leaves, halves, rank)
    offset = (me - 1) * leaves
    for t in range(leaves):
        total = None
        for j in range(entries):
            term = mm(ext[near_list[j, t] - offset], near[t, j], LAST)
            total = term if total is None else total + term
        far = None
        for j in range(entries):
            term = mm(ext_coeff[far_list[j, t] - offset], coup[t, j], LAST)
            far = term if far is None else far + term
        near_out[t] = total[:columns]
        far_out[t] = far[:columns]
        pack_rows(
            send, t, leaves, total[columns:].astype(jnp.bfloat16), far[columns:].astype(jnp.bfloat16)
        )


def down_kernel(
    node_list, upper_list, known, other, near, far, received, row, leaf_down, node_coup, node_down,
    upper_coup, upper_up, upper_down, out, *tree,
):
    half_nodes, columns, _ = known.shape
    nodes = 2 * half_nodes
    rank = row.shape[1]
    leaves = row.shape[0]
    gathered, tree = tree[0], tree[1:]
    gathered[:half_nodes] = known[...]
    gathered[half_nodes:] = other[...]
    farc = node_coup.shape[1]
    levels = nodes.bit_length() - 1
    me = lax.axis_index("leaf")

    for m in range(nodes // 2):
        left = gathered[(2 * m) ^ me, :, rank:].astype(jnp.float32)
        right = gathered[(2 * m + 1) ^ me, :, rank:].astype(jnp.float32)
        tree[levels - 2][m] = (left + right).astype(jnp.bfloat16)
    for height in range(levels - 2, 0, -1):
        breadth = 2**height
        lower = tree[height]
        for m in range(breadth):
            first = 2 * (breadth + m) - 4
            value = mm(lower[2 * m], upper_up[first], PLAIN)
            value = value + mm(lower[2 * m + 1], upper_up[first + 1], PLAIN)
            tree[height - 1][m] = value.astype(jnp.bfloat16)
    field = None
    for height in range(1, levels):
        breadth = 2**height
        node = (nodes + me) >> (levels - height)
        total = None
        for j in range(farc):
            source = tree[height - 1][upper_list[j, node - 2] - breadth]
            term = mm(source, upper_coup[node - 2, j], LAST)
            total = term if total is None else total + term
        if height > 1:
            total = total + mm(field, upper_down[node - 4], LAST)
        field = total.astype(jnp.bfloat16)
    total = mm(field, node_down[0], LAST)
    for j in range(farc):
        source = gathered[node_list[0, j] ^ me, :, :rank]
        total = total + mm(source, node_coup[0, j], LAST)
    field = total.astype(jnp.bfloat16)
    halves = near.shape[2] // 128
    for t in range(leaves):
        local = far[t] + unpack_short(received, t, leaves, halves, rank).astype(jnp.float32)
        local = (local + mm(field, leaf_down[t], LAST)).astype(jnp.bfloat16)
        close = near[t] + unpack_long(received, t, halves).astype(jnp.float32)
        out[t] = (close + mm(local, row[t], PLAIN)).astype(jnp.bfloat16)


def body(
    density,
    near_blocks,
    near_index,
    col_basis,
    row_basis,
    leaf_coupling,
    leaf_list,
    leaf_up,
    leaf_down,
    node_coupling,
    node_list,
    node_up,
    node_down,
    upper_coupling,
    upper_list,
    upper_up,
    upper_down,
):
    leaves, points, columns = density.shape
    rank = col_basis.shape[2]
    nodes = lax.axis_size("leaf")
    levels = nodes.bit_length() - 1
    bf16, f32 = jnp.bfloat16, jnp.float32
    swap = [(0, 1), (1, 0)]

    dens = jnp.swapaxes(density, 1, 2)
    coeff, message = pl.pallas_call(
        up_kernel,
        out_shape=(
            pltpu.VMEM((leaves, columns, rank), bf16),
            pltpu.VMEM((columns, 2 * rank), bf16),
        ),
        in_specs=[vmem()] * 4,
        out_specs=(vmem(), vmem()),
        name="up",
    )(dens, jnp.swapaxes(col_basis, 1, 2), leaf_up, node_up)
    tiles = leaves * (points // 128) + leaves // 2
    pack = pl.pallas_call(
        pack_kernel,
        out_shape=pltpu.VMEM((tiles, columns, 128), bf16),
        in_specs=[vmem()] * 2,
        out_specs=vmem(),
        name="pack",
    )(dens, coeff)
    staged = [near_index.T, leaf_list.T, leaf_coupling, near_blocks]
    staged = pl.pallas_call(
        stage_kernel,
        out_shape=[pltpu.VMEM(x.shape, x.dtype) for x in staged],
        in_specs=[pl.BlockSpec(memory_space=pl.ANY)] * 4,
        out_specs=[vmem()] * 4,
        scratch_shapes=[pltpu.SemaphoreType.DMA((4,))],
        name="stage",
    )(*[pltpu.with_memory_space_constraint(x, pltpu.HBM) for x in staged])
    pair = lax.ppermute(pack, "leaf", [(i, i ^ 1) for i in range(nodes)])
    others = [(i, (i + 1 if i % 2 else i - 1) % nodes) for i in range(nodes)]

    cross = lax.ppermute(pack, "leaf", others)
    own_other = lax.ppermute(pack, "sub", swap)

    entries = near_blocks.shape[1]

    def fields(*packs):
        return pl.pallas_call(
            field_kernel,
            out_shape=(
                pltpu.VMEM((leaves, columns, points), f32),
                pltpu.VMEM((leaves, columns, rank), f32),
                pltpu.VMEM((tiles, columns, 128), bf16),
            ),
            in_specs=[smem()] * 2 + [vmem()] * 8,
            out_specs=(vmem(),) * 3,
            scratch_shapes=[
                pltpu.VMEM((3 * leaves, 2 * columns, points), bf16),
                pltpu.VMEM((3 * leaves, 2 * columns, rank), bf16),
            ],
            compiler_params=pltpu.CompilerParams(vmem_limit_bytes=16 * 1024 * 1024),
            cost_estimate=pl.CostEstimate(
                flops=2 * leaves * entries * points * points * 256,
                bytes_accessed=leaves * entries * points * points * 2,
                transcendentals=0,
            ),
            name="fields",
        )(staged[0], staged[1], *packs, staged[2], staged[3])

    known = message[None]
    for bit in range(levels):
        step = 1 << bit
        other = lax.ppermute(known, "leaf", [(i, i ^ step) for i in range(nodes)])
        if bit == 0:
            known, other, pack = lax.optimization_barrier((known, other, pack))
        if bit == 1:
            known, other, pair, cross, own_other, staged = lax.optimization_barrier(
                (known, other, pair, cross, own_other, staged)
            )
            pair_other = lax.ppermute(pair, "sub", swap)
            cross_other = lax.ppermute(cross, "sub", swap)
        if bit == levels - 2:
            near, far, send = fields(pair, pack, cross, pair_other, own_other, cross_other)
            known, other, near, far, send = lax.optimization_barrier(
                (known, other, near, far, send)
            )
        if bit < levels - 1:
            known = jnp.concatenate([known, other], axis=0)
    received = lax.ppermute(send, "sub", swap)

    out = pl.pallas_call(
        down_kernel,
        out_shape=jax.ShapeDtypeStruct((leaves, columns, points), bf16),
        in_specs=[smem()] * 2 + [vmem()] * 12,
        out_specs=vmem(),
        scratch_shapes=[pltpu.VMEM((nodes, columns, 2 * rank), bf16)]
        + [pltpu.VMEM((2**height, columns, rank), bf16) for height in range(1, levels)],
        compiler_params=pltpu.CompilerParams(vmem_limit_bytes=24 * 1024 * 1024),
        name="down",
    )(
        node_list, upper_list.T, known, other, near, far, received,
        jnp.swapaxes(row_basis, 1, 2), leaf_down, node_coupling, node_down, upper_coupling, upper_up, upper_down,
    )
    return jnp.swapaxes(out, 1, 2)


def solution(mesh):
    placed = (
        P("leaf", None, "sub"),
        P("leaf", "sub", None, None),
        P("leaf", "sub"),
        P("leaf", None, None),
        P("leaf", None, None),
        P("leaf", "sub", None, None),
        P("leaf", "sub"),
        P("leaf", None, None),
        P("leaf", None, None),
        P("leaf", None, None, None),
        P("leaf", None),
        P("leaf", None, None),
        P("leaf", None, None),
        P(),
        P(),
        P(),
        P(),
    )
    return jax.shard_map(
        body, mesh=mesh, in_specs=placed, out_specs=P("leaf", None, "sub"), check_vma=False
    )
```

```python
import jax
import jax.numpy as jnp
from jax import lax
from jax.experimental import pallas as pl
from jax.experimental.pallas import tpu as pltpu
from jax.sharding import PartitionSpec as P

LAST = (((1,), (1,)), ((), ()))
PLAIN = (((1,), (0,)), ((), ()))


def mm(a, b, dims):
    return lax.dot_general(a, b, dims, preferred_element_type=jnp.float32)


def pinned(x, space):
    return pltpu.with_memory_space_constraint(x, space)


def limit(mebibytes):
    return pltpu.CompilerParams(vmem_limit_bytes=mebibytes * 1024 * 1024)


def vmem():
    return pl.BlockSpec(memory_space=pltpu.VMEM)


def smem():
    return pl.BlockSpec(memory_space=pltpu.SMEM)


def up_kernel(dens, col, leaf_up, node_up, coeff_out, message, dens_out):
    leaves = dens.shape[0]
    dens_out[...] = dens[...]
    rank = col.shape[1]
    node = None
    for t in range(leaves):
        coeff = mm(dens[t], col[t], LAST).astype(jnp.bfloat16)
        coeff_out[t] = coeff
        term = mm(coeff, leaf_up[t], PLAIN)
        node = term if node is None else node + term
    node = node.astype(jnp.bfloat16)
    message[:, :rank] = node
    message[:, rank:] = mm(node, node_up[0], PLAIN).astype(jnp.bfloat16)


def pack_rows(pack, t, leaves, long, short):
    halves = long.shape[1] // 128
    rank = short.shape[1]
    for h in range(halves):
        pack[t * halves + h] = long[:, h * 128 : (h + 1) * 128]
    side = t % 2
    pack[leaves * halves + t // 2, :, side * rank : (side + 1) * rank] = short


def unpack_long(pack, t, halves):
    return jnp.concatenate([pack[t * halves + h] for h in range(halves)], axis=1)


def unpack_short(pack, t, leaves, halves, rank):
    side = t % 2
    return pack[leaves * halves + t // 2, :, side * rank : (side + 1) * rank]


def pack_kernel(dens, coeff, pack):
    leaves = dens.shape[0]
    for t in range(leaves):
        pack_rows(pack, t, leaves, dens[t], coeff[t])


def stage_kernel(*refs):
    count = len(refs) // 2
    sems = refs[-1]
    copies = [
        pltpu.make_async_copy(source, target, sems.at[k])
        for k, (source, target) in enumerate(zip(refs[:count], refs[count:-1]))
    ]
    for copy in copies:
        copy.start()
    for copy in copies:
        copy.wait()


def field_kernel(
    near_list, far_list, pair, own, cross, pair_other, own_other, cross_other, coup, near,
    near_out, far_out, send, ext, ext_coeff,
):
    leaves, entries = near.shape[0], near.shape[1]
    columns = own.shape[1]
    rank = coup.shape[-1]
    halves = near.shape[-1] // 128
    me = lax.axis_index("leaf")
    odd = me & 1
    for slot, pair_of_cores in (
        (2 - 2 * odd, (pair, pair_other)),
        (1, (own, own_other)),
        (2 * odd, (cross, cross_other)),
    ):
        for c, ref in enumerate(pair_of_cores):
            rows = slice(c * columns, (c + 1) * columns)
            for t in range(leaves):
                ext[slot * leaves + t, rows] = unpack_long(ref, t, halves)
                ext_coeff[slot * leaves + t, rows] = unpack_short(ref, t, leaves, halves, rank)
    offset = (me - 1) * leaves
    for t in range(leaves):
        total = None
        for j in range(entries):
            term = mm(ext[near_list[j, t] - offset], near[t, j], LAST)
            total = term if total is None else total + term
        far = None
        for j in range(entries):
            term = mm(ext_coeff[far_list[j, t] - offset], coup[t, j], LAST)
            far = term if far is None else far + term
        near_out[t] = total[:columns]
        far_out[t] = far[:columns]
        pack_rows(
            send, t, leaves, total[columns:].astype(jnp.bfloat16), far[columns:].astype(jnp.bfloat16)
        )


def down_kernel(
    node_list, upper_list, known, other, near, far, received, row, leaf_down, node_coup, node_down,
    upper_coup, upper_up, upper_down, out, *tree,
):
    half_nodes, columns, _ = known.shape
    nodes = 2 * half_nodes
    rank = row.shape[1]
    leaves = row.shape[0]
    gathered, tree = tree[0], tree[1:]
    gathered[:half_nodes] = known[...]
    gathered[half_nodes:] = other[...]
    farc = node_coup.shape[1]
    levels = nodes.bit_length() - 1
    me = lax.axis_index("leaf")

    for m in range(nodes // 2):
        left = gathered[(2 * m) ^ me, :, rank:].astype(jnp.float32)
        right = gathered[(2 * m + 1) ^ me, :, rank:].astype(jnp.float32)
        tree[levels - 2][m] = (left + right).astype(jnp.bfloat16)
    for height in range(levels - 2, 0, -1):
        breadth = 2**height
        lower = tree[height]
        for m in range(breadth):
            first = 2 * (breadth + m) - 4
            value = mm(lower[2 * m], upper_up[first], PLAIN)
            value = value + mm(lower[2 * m + 1], upper_up[first + 1], PLAIN)
            tree[height - 1][m] = value.astype(jnp.bfloat16)
    field = None
    for height in range(1, levels):
        breadth = 2**height
        node = (nodes + me) >> (levels - height)
        total = None
        for j in range(farc):
            source = tree[height - 1][upper_list[j, node - 2] - breadth]
            term = mm(source, upper_coup[node - 2, j], LAST)
            total = term if total is None else total + term
        if height > 1:
            total = total + mm(field, upper_down[node - 4], LAST)
        field = total.astype(jnp.bfloat16)
    total = mm(field, node_down[0], LAST)
    for j in range(farc):
        source = gathered[node_list[0, j] ^ me, :, :rank]
        total = total + mm(source, node_coup[0, j], LAST)
    field = total.astype(jnp.bfloat16)
    halves = near.shape[2] // 128
    for t in range(leaves):
        local = far[t] + unpack_short(received, t, leaves, halves, rank).astype(jnp.float32)
        local = (local + mm(field, leaf_down[t], LAST)).astype(jnp.bfloat16)
        close = near[t] + unpack_long(received, t, halves).astype(jnp.float32)
        out[t] = (close + mm(local, row[t], PLAIN)).astype(jnp.bfloat16)


def body(
    density,
    near_blocks,
    near_index,
    col_basis,
    row_basis,
    leaf_coupling,
    leaf_list,
    leaf_up,
    leaf_down,
    node_coupling,
    node_list,
    node_up,
    node_down,
    upper_coupling,
    upper_list,
    upper_up,
    upper_down,
):
    leaves, points, columns = density.shape
    rank = col_basis.shape[2]
    nodes = lax.axis_size("leaf")
    levels = nodes.bit_length() - 1
    bf16, f32 = jnp.bfloat16, jnp.float32
    swap = [(0, 1), (1, 0)]

    dens = jnp.swapaxes(density, 1, 2)
    coeff, message, dens_here = pl.pallas_call(
        up_kernel,
        out_shape=(
            pltpu.VMEM((leaves, columns, rank), bf16),
            pltpu.VMEM((columns, 2 * rank), bf16),
            pltpu.VMEM(dens.shape, bf16),
        ),
        in_specs=[vmem()] * 4,
        out_specs=(vmem(),) * 3,
        compiler_params=limit(4),
        name="up",
    )(*[pinned(x, pltpu.HBM) for x in (dens, jnp.swapaxes(col_basis, 1, 2), leaf_up, node_up)])
    tiles = leaves * (points // 128) + leaves // 2
    pack = pl.pallas_call(
        pack_kernel,
        out_shape=pltpu.VMEM((tiles, columns, 128), bf16),
        in_specs=[vmem()] * 2,
        out_specs=vmem(),
        compiler_params=limit(4),
        name="pack",
    )(pinned(dens_here, pltpu.VMEM), pinned(coeff, pltpu.VMEM))
    staged = [near_index.T, leaf_list.T, leaf_coupling, near_blocks]
    staged = pl.pallas_call(
        stage_kernel,
        out_shape=[pltpu.VMEM(x.shape, x.dtype) for x in staged],
        in_specs=[pl.BlockSpec(memory_space=pl.ANY)] * 4,
        out_specs=[vmem()] * 4,
        scratch_shapes=[pltpu.SemaphoreType.DMA((4,))],
        compiler_params=limit(4),
        name="stage",
    )(*[pinned(x, pltpu.HBM) for x in staged])
    pair = lax.ppermute(pack, "leaf", [(i, i ^ 1) for i in range(nodes)])
    cores = lax.axis_size("sub")
    others = [
        (i * cores + c, (i + 1 if i % 2 else i - 1) * cores + c)
        for i in range(1, nodes - 1)
        for c in range(cores)
    ]
    others += [(i * cores + c, i * cores + 1 - c) for i in (0, nodes - 1) for c in range(cores)]

    cross = lax.ppermute(pack, ("leaf", "sub"), others)
    own_other = lax.ppermute(pack, "sub", swap)

    entries = near_blocks.shape[1]

    def fields(*packs):
        return pl.pallas_call(
            field_kernel,
            out_shape=(
                pltpu.VMEM((leaves, columns, points), f32),
                pltpu.VMEM((leaves, columns, rank), f32),
                pltpu.VMEM((tiles, columns, 128), bf16),
            ),
            in_specs=[smem()] * 2 + [vmem()] * 8,
            out_specs=(vmem(),) * 3,
            scratch_shapes=[
                pltpu.VMEM((3 * leaves, 2 * columns, points), bf16),
                pltpu.VMEM((3 * leaves, 2 * columns, rank), bf16),
            ],
            compiler_params=limit(8),
            cost_estimate=pl.CostEstimate(
                flops=2 * leaves * entries * points * points * 256,
                bytes_accessed=leaves * entries * points * points * 2,
                transcendentals=0,
            ),
            name="fields",
        )(staged[0], staged[1], *packs, staged[2], staged[3])

    known = message[None]
    for bit in range(levels):
        step = 1 << bit
        other = lax.ppermute(known, "leaf", [(i, i ^ step) for i in range(nodes)])
        if bit == 0:
            known, other, pack = lax.optimization_barrier((known, other, pack))
        if bit == 1:
            known, other, pair, cross, own_other, staged = lax.optimization_barrier(
                (known, other, pair, cross, own_other, staged)
            )
            pair_other = lax.ppermute(pair, "sub", swap)
            cross_other = lax.ppermute(cross, "sub", swap)
        if bit == levels - 2:
            near, far, send = fields(pair, pack, cross, pair_other, own_other, cross_other)
            known, other, near, far, send = lax.optimization_barrier(
                (known, other, near, far, send)
            )
        if bit < levels - 1:
            known = jnp.concatenate([known, other], axis=0)
    received = lax.ppermute(send, "sub", swap)

    out = pl.pallas_call(
        down_kernel,
        out_shape=jax.ShapeDtypeStruct((leaves, columns, points), bf16),
        in_specs=[smem()] * 2 + [vmem()] * 12,
        out_specs=vmem(),
        scratch_shapes=[pltpu.VMEM((nodes, columns, 2 * rank), bf16)]
        + [pltpu.VMEM((2**height, columns, rank), bf16) for height in range(1, levels)],
        compiler_params=limit(8),
        name="down",
    )(
        node_list, upper_list.T, known, other, near, far, received,
        jnp.swapaxes(row_basis, 1, 2), leaf_down, node_coupling, node_down, upper_coupling, upper_up, upper_down,
    )
    return jnp.swapaxes(out, 1, 2)


def solution(mesh):
    placed = (
        P("leaf", None, "sub"),
        P("leaf", "sub", None, None),
        P("leaf", "sub"),
        P("leaf", None, None),
        P("leaf", None, None),
        P("leaf", "sub", None, None),
        P("leaf", "sub"),
        P("leaf", None, None),
        P("leaf", None, None),
        P("leaf", None, None, None),
        P("leaf", None),
        P("leaf", None, None),
        P("leaf", None, None),
        P(),
        P(),
        P(),
        P(),
    )
    return jax.shard_map(
        body, mesh=mesh, in_specs=placed, out_specs=P("leaf", None, "sub"), check_vma=False
    )
```

```python
import jax
import jax.numpy as jnp
from jax import lax
from jax.experimental import pallas as pl
from jax.experimental.pallas import tpu as pltpu
from jax.sharding import PartitionSpec as P

LAST = (((1,), (1,)), ((), ()))
PLAIN = (((1,), (0,)), ((), ()))


def mm(a, b, dims):
    return lax.dot_general(a, b, dims, preferred_element_type=jnp.float32)


def pinned(x, space):
    return pltpu.with_memory_space_constraint(x, space)


def limit(mebibytes):
    return pltpu.CompilerParams(vmem_limit_bytes=mebibytes * 1024 * 1024)


def vmem():
    return pl.BlockSpec(memory_space=pltpu.VMEM)


def smem():
    return pl.BlockSpec(memory_space=pltpu.SMEM)


def up_kernel(dens, col, leaf_up, node_up, coeff_out, message, dens_out):
    leaves = dens.shape[0]
    dens_out[...] = dens[...]
    rank = col.shape[1]
    node = None
    for t in range(leaves):
        coeff = mm(dens[t], col[t], LAST).astype(jnp.bfloat16)
        coeff_out[t] = coeff
        term = mm(coeff, leaf_up[t], PLAIN)
        node = term if node is None else node + term
    node = node.astype(jnp.bfloat16)
    message[:, :rank] = node
    message[:, rank:] = mm(node, node_up[0], PLAIN).astype(jnp.bfloat16)


def pack_rows(pack, t, leaves, long, short):
    halves = long.shape[1] // 128
    rank = short.shape[1]
    for h in range(halves):
        pack[t * halves + h] = long[:, h * 128 : (h + 1) * 128]
    side = t % 2
    pack[leaves * halves + t // 2, :, side * rank : (side + 1) * rank] = short


def unpack_long(pack, t, halves):
    return jnp.concatenate([pack[t * halves + h] for h in range(halves)], axis=1)


def unpack_short(pack, t, leaves, halves, rank):
    side = t % 2
    return pack[leaves * halves + t // 2, :, side * rank : (side + 1) * rank]


def pack_kernel(dens, coeff, pack):
    leaves = dens.shape[0]
    for t in range(leaves):
        pack_rows(pack, t, leaves, dens[t], coeff[t])


def stage_kernel(*refs):
    count = len(refs) // 2
    sems = refs[-1]
    copies = [
        pltpu.make_async_copy(source, target, sems.at[k])
        for k, (source, target) in enumerate(zip(refs[:count], refs[count:-1]))
    ]
    for copy in copies:
        copy.start()
    for copy in copies:
        copy.wait()


def field_kernel(
    near_list, far_list, pair, own, cross, pair_other, own_other, cross_other, coup, near,
    near_out, far_out, send, ext, ext_coeff,
):
    leaves, entries = near.shape[0], near.shape[1]
    columns = own.shape[1]
    rank = coup.shape[-1]
    halves = near.shape[-1] // 128
    me = lax.axis_index("leaf")
    odd = me & 1
    for slot, pair_of_cores in (
        (2 - 2 * odd, (pair, pair_other)),
        (1, (own, own_other)),
        (2 * odd, (cross, cross_other)),
    ):
        for c, ref in enumerate(pair_of_cores):
            rows = slice(c * columns, (c + 1) * columns)
            for t in range(leaves):
                ext[slot * leaves + t, rows] = unpack_long(ref, t, halves)
                ext_coeff[slot * leaves + t, rows] = unpack_short(ref, t, leaves, halves, rank)
    offset = (me - 1) * leaves
    for t in range(leaves):
        total = None
        for j in range(entries):
            term = mm(ext[near_list[j, t] - offset], near[t, j], LAST)
            total = term if total is None else total + term
        far = None
        for j in range(entries):
            term = mm(ext_coeff[far_list[j, t] - offset], coup[t, j], LAST)
            far = term if far is None else far + term
        near_out[t] = total[:columns]
        far_out[t] = far[:columns]
        pack_rows(
            send, t, leaves, total[columns:].astype(jnp.bfloat16), far[columns:].astype(jnp.bfloat16)
        )


def weights_kernel(
    node_list, upper_list, node_coup, node_down, upper_coup, upper_up, upper_down, leaf_down, row,
    to_field, to_points, named, *tree,
):
    nodes, rank = to_field.shape[0], to_field.shape[1]
    farc = node_coup.shape[1]
    levels = nodes.bit_length() - 1
    me = lax.axis_index("leaf")
    for t in range(leaf_down.shape[0]):
        to_points[t] = mm(leaf_down[t], row[t], (((0,), (0,)), ((), ()))).astype(jnp.bfloat16)
    named[...] = jnp.zeros_like(named)
    for j in range(farc):
        place = node_list[0, j] ^ me
        named[place] = named[place] + node_coup[0, j].astype(jnp.float32)
    for height in range(1, levels):
        breadth = 2**height
        node = (nodes + me) >> (levels - height)
        level = tree[height - 1]
        level[...] = jnp.zeros_like(level)
        for j in range(farc):
            place = upper_list[j, node - 2] - breadth
            level[place] = level[place] + upper_coup[node - 2, j].astype(jnp.float32)
        if height > 1:
            for parent in range(breadth // 2):
                above = tree[height - 2][parent].astype(jnp.bfloat16)
                above = mm(upper_down[node - 4], above, PLAIN).astype(jnp.bfloat16)
                for m in (2 * parent, 2 * parent + 1):
                    level[m] = level[m] + mm(above, upper_up[breadth + m - 4], LAST)
    for parent in range(nodes // 2):
        lifted = mm(node_down[0], tree[levels - 2][parent].astype(jnp.bfloat16), PLAIN)
        lifted = lifted.astype(jnp.bfloat16)
        for n in (2 * parent, 2 * parent + 1):
            to_field[n ^ me, :, rank:] = lifted
    for place in range(nodes):
        to_field[place, :, :rank] = named[place].astype(jnp.bfloat16)


def base_kernel(near, far, received, row, base):
    leaves, rank = row.shape[0], row.shape[1]
    halves = near.shape[2] // 128
    for t in range(leaves):
        local = far[t] + unpack_short(received, t, leaves, halves, rank).astype(jnp.float32)
        close = near[t] + unpack_long(received, t, halves).astype(jnp.float32)
        base[t] = close + mm(local.astype(jnp.bfloat16), row[t], PLAIN)


def down_kernel(known, other, to_field, to_points, base, out):
    half = known.shape[0]
    messages = [known[p] for p in range(half)] + [other[p] for p in range(half)]
    matrices = [to_field[p] for p in range(2 * half)]
    field = mm(jnp.concatenate(messages, axis=1), jnp.concatenate(matrices, axis=1), LAST)
    field = field.astype(jnp.bfloat16)
    for t in range(out.shape[0]):
        out[t] = (base[t] + mm(field, to_points[t], PLAIN)).astype(jnp.bfloat16)


def body(
    density,
    near_blocks,
    near_index,
    col_basis,
    row_basis,
    leaf_coupling,
    leaf_list,
    leaf_up,
    leaf_down,
    node_coupling,
    node_list,
    node_up,
    node_down,
    upper_coupling,
    upper_list,
    upper_up,
    upper_down,
):
    leaves, points, columns = density.shape
    rank = col_basis.shape[2]
    nodes = lax.axis_size("leaf")
    levels = nodes.bit_length() - 1
    bf16, f32 = jnp.bfloat16, jnp.float32
    swap = [(0, 1), (1, 0)]

    dens = jnp.swapaxes(density, 1, 2)
    coeff, message, dens_here = pl.pallas_call(
        up_kernel,
        out_shape=(
            pltpu.VMEM((leaves, columns, rank), bf16),
            pltpu.VMEM((columns, 2 * rank), bf16),
            pltpu.VMEM(dens.shape, bf16),
        ),
        in_specs=[vmem()] * 4,
        out_specs=(vmem(),) * 3,
        compiler_params=limit(4),
        cost_estimate=pl.CostEstimate(
            flops=2_000_000_000, bytes_accessed=5_000_000, transcendentals=0
        ),
        name="up",
    )(*[pinned(x, pltpu.HBM) for x in (dens, jnp.swapaxes(col_basis, 1, 2), leaf_up, node_up)])
    tiles = leaves * (points // 128) + leaves // 2
    pack = pl.pallas_call(
        pack_kernel,
        out_shape=pltpu.VMEM((tiles, columns, 128), bf16),
        in_specs=[vmem()] * 2,
        out_specs=vmem(),
        compiler_params=limit(4),
        cost_estimate=pl.CostEstimate(
            flops=2_000_000_000, bytes_accessed=5_000_000, transcendentals=0
        ),
        name="pack",
    )(pinned(dens_here, pltpu.VMEM), pinned(coeff, pltpu.VMEM))
    staged = (near_index.T, leaf_list.T, leaf_coupling, near_blocks)
    cores = lax.axis_size("sub")
    others = [
        (i * cores + c, (i + 1 if i % 2 else i - 1) * cores + c)
        for i in range(1, nodes - 1)
        for c in range(cores)
    ]
    others += [(i * cores + c, i * cores + 1 - c) for i in (0, nodes - 1) for c in range(cores)]

    cross = lax.ppermute(pack, ("leaf", "sub"), others)

    entries = near_blocks.shape[1]

    def fields(*packs):
        return pl.pallas_call(
            field_kernel,
            out_shape=(
                pltpu.VMEM((leaves, columns, points), f32),
                pltpu.VMEM((leaves, columns, rank), f32),
                pltpu.VMEM((tiles, columns, 128), bf16),
            ),
            in_specs=[smem()] * 2 + [vmem()] * 8,
            out_specs=(vmem(),) * 3,
            scratch_shapes=[
                pltpu.VMEM((3 * leaves, 2 * columns, points), bf16),
                pltpu.VMEM((3 * leaves, 2 * columns, rank), bf16),
            ],
            compiler_params=limit(8),
            cost_estimate=pl.CostEstimate(
                flops=2 * leaves * entries * points * points * 256,
                bytes_accessed=leaves * entries * points * points * 2,
                transcendentals=0,
            ),
            name="fields",
        )(staged[0], staged[1], *packs, staged[2], staged[3])

    row = jnp.swapaxes(row_basis, 1, 2)
    weights = pl.pallas_call(
        weights_kernel,
        out_shape=(
            pltpu.VMEM((nodes, rank, 2 * rank), bf16),
            pltpu.VMEM((leaves, rank, points), bf16),
        ),
        in_specs=[smem()] * 2 + [vmem()] * 7,
        out_specs=(vmem(),) * 2,
        scratch_shapes=[pltpu.VMEM((nodes, rank, rank), f32)]
        + [pltpu.VMEM((2**height, rank, rank), f32) for height in range(1, levels)],
        compiler_params=limit(16),
        cost_estimate=pl.CostEstimate(
            flops=2_000_000_000, bytes_accessed=3_000_000, transcendentals=0
        ),
        name="weights",
    )(
        node_list, upper_list.T, node_coupling, node_down, upper_coupling, upper_up, upper_down,
        leaf_down, row,
    )

    known = message[None]
    for bit in range(levels):
        step = 1 << bit
        other = lax.ppermute(known, "leaf", [(i, i ^ step) for i in range(nodes)])
        if bit == 0:
            known, other, pack = lax.optimization_barrier((known, other, pack))
            pair = lax.ppermute(pack, "leaf", [(i, i ^ 1) for i in range(nodes)])
            own_other = lax.ppermute(pack, "sub", swap)
        if bit == 1:
            known, other, pair, cross, own_other, weights = lax.optimization_barrier(
                (known, other, pair, cross, own_other, weights)
            )
            pair_other = lax.ppermute(pair, "sub", swap)
            cross_other = lax.ppermute(cross, "sub", swap)
        if bit == levels - 2:
            near, far, send = fields(pair, pack, cross, pair_other, own_other, cross_other)
            known, other, near, far, send = lax.optimization_barrier(
                (known, other, near, far, send)
            )
        if bit < levels - 1:
            known = jnp.concatenate([known, other], axis=0)
    received = lax.ppermute(send, "sub", swap)
    base = pl.pallas_call(
        base_kernel,
        out_shape=pltpu.VMEM((leaves, columns, points), f32),
        in_specs=[vmem()] * 4,
        out_specs=vmem(),
        compiler_params=limit(4),
        cost_estimate=pl.CostEstimate(
            flops=1_000_000_000, bytes_accessed=1_000_000, transcendentals=0
        ),
        name="base",
    )(near, far, received, row)
    other, base = lax.optimization_barrier((other, base))
    out = pl.pallas_call(
        down_kernel,
        out_shape=jax.ShapeDtypeStruct((leaves, columns, points), bf16),
        in_specs=[vmem()] * 5,
        out_specs=vmem(),
        compiler_params=limit(8),
        name="down",
    )(known, other, *weights, base)
    return jnp.swapaxes(out, 1, 2)


def solution(mesh):
    placed = (
        P("leaf", None, "sub"),
        P("leaf", "sub", None, None),
        P("leaf", "sub"),
        P("leaf", None, None),
        P("leaf", None, None),
        P("leaf", "sub", None, None),
        P("leaf", "sub"),
        P("leaf", None, None),
        P("leaf", None, None),
        P("leaf", None, None, None),
        P("leaf", None),
        P("leaf", None, None),
        P("leaf", None, None),
        P(),
        P(),
        P(),
        P(),
    )
    return jax.shard_map(
        body, mesh=mesh, in_specs=placed, out_specs=P("leaf", None, "sub"), check_vma=False
    )
```

```python
import jax
import jax.numpy as jnp
from jax import lax
from jax.experimental import pallas as pl
from jax.experimental.pallas import tpu as pltpu
from jax.sharding import PartitionSpec as P

LAST = (((1,), (1,)), ((), ()))
PLAIN = (((1,), (0,)), ((), ()))


def mm(a, b, dims):
    return lax.dot_general(a, b, dims, preferred_element_type=jnp.float32)


def pinned(x, space):
    return pltpu.with_memory_space_constraint(x, space)


def limit(mebibytes):
    return pltpu.CompilerParams(vmem_limit_bytes=mebibytes * 1024 * 1024)


def vmem():
    return pl.BlockSpec(memory_space=pltpu.VMEM)


def smem():
    return pl.BlockSpec(memory_space=pltpu.SMEM)


def up_kernel(dens, col, leaf_up, node_up, coeff_out, message, dens_out):
    leaves = dens.shape[0]
    dens_out[...] = dens[...]
    rank = col.shape[1]
    node = None
    for t in range(leaves):
        coeff = mm(dens[t], col[t], LAST).astype(jnp.bfloat16)
        coeff_out[t] = coeff
        term = mm(coeff, leaf_up[t], PLAIN)
        node = term if node is None else node + term
    node = node.astype(jnp.bfloat16)
    message[:, :rank] = node
    message[:, rank:] = mm(node, node_up[0], PLAIN).astype(jnp.bfloat16)


def pack_rows(pack, t, leaves, long, short):
    halves = long.shape[1] // 128
    rank = short.shape[1]
    for h in range(halves):
        pack[t * halves + h] = long[:, h * 128 : (h + 1) * 128]
    side = t % 2
    pack[leaves * halves + t // 2, :, side * rank : (side + 1) * rank] = short


def unpack_long(pack, t, halves):
    return jnp.concatenate([pack[t * halves + h] for h in range(halves)], axis=1)


def unpack_short(pack, t, leaves, halves, rank):
    side = t % 2
    return pack[leaves * halves + t // 2, :, side * rank : (side + 1) * rank]


def pack_kernel(dens, coeff, pack):
    leaves = dens.shape[0]
    for t in range(leaves):
        pack_rows(pack, t, leaves, dens[t], coeff[t])


def stage_kernel(*refs):
    count = len(refs) // 2
    sems = refs[-1]
    copies = [
        pltpu.make_async_copy(source, target, sems.at[k])
        for k, (source, target) in enumerate(zip(refs[:count], refs[count:-1]))
    ]
    for copy in copies:
        copy.start()
    for copy in copies:
        copy.wait()


def field_kernel(
    near_list, far_list, pair, own, cross, pair_other, own_other, cross_other, coup, near,
    near_out, far_out, send, ext, ext_coeff,
):
    leaves, entries = near.shape[0], near.shape[1]
    columns = own.shape[1]
    rank = coup.shape[-1]
    halves = near.shape[-1] // 128
    me = lax.axis_index("leaf")
    odd = me & 1
    for slot, pair_of_cores in (
        (2 - 2 * odd, (pair, pair_other)),
        (1, (own, own_other)),
        (2 * odd, (cross, cross_other)),
    ):
        for c, ref in enumerate(pair_of_cores):
            rows = slice(c * columns, (c + 1) * columns)
            for t in range(leaves):
                ext[slot * leaves + t, rows] = unpack_long(ref, t, halves)
                ext_coeff[slot * leaves + t, rows] = unpack_short(ref, t, leaves, halves, rank)
    offset = (me - 1) * leaves
    for t in range(leaves):
        total = None
        for j in range(entries):
            term = mm(ext[near_list[j, t] - offset], near[t, j], LAST)
            total = term if total is None else total + term
        far = None
        for j in range(entries):
            term = mm(ext_coeff[far_list[j, t] - offset], coup[t, j], LAST)
            far = term if far is None else far + term
        near_out[t] = total[:columns]
        far_out[t] = far[:columns]
        pack_rows(
            send, t, leaves, total[columns:].astype(jnp.bfloat16), far[columns:].astype(jnp.bfloat16)
        )


def weights_kernel(
    node_list, upper_list, node_coup, node_down, upper_coup, upper_up, upper_down, leaf_down, row,
    to_field, to_points, named, *tree,
):
    nodes, rank = to_field.shape[0], to_field.shape[1]
    farc = node_coup.shape[1]
    levels = nodes.bit_length() - 1
    me = lax.axis_index("leaf")
    for t in range(leaf_down.shape[0]):
        to_points[t] = mm(leaf_down[t], row[t], (((0,), (0,)), ((), ()))).astype(jnp.bfloat16)
    named[...] = jnp.zeros_like(named)
    for j in range(farc):
        place = node_list[0, j] ^ me
        named[place] = named[place] + node_coup[0, j].astype(jnp.float32)
    for height in range(1, levels):
        breadth = 2**height
        node = (nodes + me) >> (levels - height)
        level = tree[height - 1]
        level[...] = jnp.zeros_like(level)
        for j in range(farc):
            place = upper_list[j, node - 2] - breadth
            level[place] = level[place] + upper_coup[node - 2, j].astype(jnp.float32)
        if height > 1:
            for parent in range(breadth // 2):
                above = tree[height - 2][parent].astype(jnp.bfloat16)
                above = mm(upper_down[node - 4], above, PLAIN).astype(jnp.bfloat16)
                for m in (2 * parent, 2 * parent + 1):
                    level[m] = level[m] + mm(above, upper_up[breadth + m - 4], LAST)
    for parent in range(nodes // 2):
        lifted = mm(node_down[0], tree[levels - 2][parent].astype(jnp.bfloat16), PLAIN)
        lifted = lifted.astype(jnp.bfloat16)
        for n in (2 * parent, 2 * parent + 1):
            to_field[n ^ me, :, rank:] = lifted
    for place in range(nodes):
        to_field[place, :, :rank] = named[place].astype(jnp.bfloat16)


def base_kernel(near, far, received, row, base):
    leaves, rank = row.shape[0], row.shape[1]
    halves = near.shape[2] // 128
    for t in range(leaves):
        local = far[t] + unpack_short(received, t, leaves, halves, rank).astype(jnp.float32)
        close = near[t] + unpack_long(received, t, halves).astype(jnp.float32)
        base[t] = close + mm(local.astype(jnp.bfloat16), row[t], PLAIN)


def down_kernel(known, other, to_field, to_points, base, out):
    half = known.shape[0]
    messages = [known[p] for p in range(half)] + [other[p] for p in range(half)]
    matrices = [to_field[p] for p in range(2 * half)]
    field = mm(jnp.concatenate(messages, axis=1), jnp.concatenate(matrices, axis=1), LAST)
    field = field.astype(jnp.bfloat16)
    for t in range(out.shape[0]):
        out[t] = (base[t] + mm(field, to_points[t], PLAIN)).astype(jnp.bfloat16)


def body(
    density,
    near_blocks,
    near_index,
    col_basis,
    row_basis,
    leaf_coupling,
    leaf_list,
    leaf_up,
    leaf_down,
    node_coupling,
    node_list,
    node_up,
    node_down,
    upper_coupling,
    upper_list,
    upper_up,
    upper_down,
):
    leaves, points, columns = density.shape
    rank = col_basis.shape[2]
    nodes = lax.axis_size("leaf")
    levels = nodes.bit_length() - 1
    bf16, f32 = jnp.bfloat16, jnp.float32
    swap = [(0, 1), (1, 0)]

    dens = jnp.swapaxes(density, 1, 2)
    coeff, message, dens_here = pl.pallas_call(
        up_kernel,
        out_shape=(
            pltpu.VMEM((leaves, columns, rank), bf16),
            pltpu.VMEM((columns, 2 * rank), bf16),
            pltpu.VMEM(dens.shape, bf16),
        ),
        in_specs=[vmem()] * 4,
        out_specs=(vmem(),) * 3,
        compiler_params=limit(4),
        cost_estimate=pl.CostEstimate(
            flops=2_000_000_000, bytes_accessed=5_000_000, transcendentals=0
        ),
        name="up",
    )(*[pinned(x, pltpu.HBM) for x in (dens, jnp.swapaxes(col_basis, 1, 2), leaf_up, node_up)])
    tiles = leaves * (points // 128) + leaves // 2
    pack = pl.pallas_call(
        pack_kernel,
        out_shape=pltpu.VMEM((tiles, columns, 128), bf16),
        in_specs=[vmem()] * 2,
        out_specs=vmem(),
        compiler_params=limit(4),
        cost_estimate=pl.CostEstimate(
            flops=2_000_000_000, bytes_accessed=5_000_000, transcendentals=0
        ),
        name="pack",
    )(pinned(dens_here, pltpu.VMEM), pinned(coeff, pltpu.VMEM))
    staged = (near_index.T, leaf_list.T, leaf_coupling, near_blocks)
    cores = lax.axis_size("sub")
    others = [
        (i * cores + c, (i + 1 if i % 2 else i - 1) * cores + c)
        for i in range(1, nodes - 1)
        for c in range(cores)
    ]
    others += [(i * cores + c, i * cores + 1 - c) for i in (0, nodes - 1) for c in range(cores)]

    cross = lax.ppermute(pack, ("leaf", "sub"), others)
    pair = lax.ppermute(pack, "leaf", [(i, i ^ 1) for i in range(nodes)])
    own_other = lax.ppermute(pack, "sub", swap)

    entries = near_blocks.shape[1]

    def fields(*packs):
        return pl.pallas_call(
            field_kernel,
            out_shape=(
                pltpu.VMEM((leaves, columns, points), f32),
                pltpu.VMEM((leaves, columns, rank), f32),
                pltpu.VMEM((tiles, columns, 128), bf16),
            ),
            in_specs=[smem()] * 2 + [vmem()] * 8,
            out_specs=(vmem(),) * 3,
            scratch_shapes=[
                pltpu.VMEM((3 * leaves, 2 * columns, points), bf16),
                pltpu.VMEM((3 * leaves, 2 * columns, rank), bf16),
            ],
            compiler_params=limit(8),
            cost_estimate=pl.CostEstimate(
                flops=2 * leaves * entries * points * points * 256,
                bytes_accessed=leaves * entries * points * points * 2,
                transcendentals=0,
            ),
            name="fields",
        )(staged[0], staged[1], *packs, staged[2], staged[3])

    row = jnp.swapaxes(row_basis, 1, 2)
    weights = pl.pallas_call(
        weights_kernel,
        out_shape=(
            pltpu.VMEM((nodes, rank, 2 * rank), bf16),
            pltpu.VMEM((leaves, rank, points), bf16),
        ),
        in_specs=[smem()] * 2 + [vmem()] * 7,
        out_specs=(vmem(),) * 2,
        scratch_shapes=[pltpu.VMEM((nodes, rank, rank), f32)]
        + [pltpu.VMEM((2**height, rank, rank), f32) for height in range(1, levels)],
        compiler_params=limit(16),
        cost_estimate=pl.CostEstimate(
            flops=2_000_000_000, bytes_accessed=3_000_000, transcendentals=0
        ),
        name="weights",
    )(
        node_list, upper_list.T, node_coupling, node_down, upper_coupling, upper_up, upper_down,
        leaf_down, row,
    )

    known = message[None]
    for bit in range(levels):
        step = 1 << bit
        other = lax.ppermute(known, "leaf", [(i, i ^ step) for i in range(nodes)])
        if bit == 0:
            known, other, pack = lax.optimization_barrier((known, other, pack))
        if bit == 1:
            known, other, cross, pair, own_other, weights = lax.optimization_barrier(
                (known, other, cross, pair, own_other, weights)
            )
            pair_other = lax.ppermute(pair, "sub", swap)
            cross_other = lax.ppermute(cross, "sub", swap)
        if bit == levels - 2:
            near, far, send = fields(pair, pack, cross, pair_other, own_other, cross_other)
            known, other, near, far, send = lax.optimization_barrier(
                (known, other, near, far, send)
            )
        if bit < levels - 1:
            known = jnp.concatenate([known, other], axis=0)
    received = lax.ppermute(send, "sub", swap)
    base = pl.pallas_call(
        base_kernel,
        out_shape=pltpu.VMEM((leaves, columns, points), f32),
        in_specs=[vmem()] * 4,
        out_specs=vmem(),
        compiler_params=limit(4),
        cost_estimate=pl.CostEstimate(
            flops=1_000_000_000, bytes_accessed=1_000_000, transcendentals=0
        ),
        name="base",
    )(near, far, received, row)
    other, base = lax.optimization_barrier((other, base))
    out = pl.pallas_call(
        down_kernel,
        out_shape=jax.ShapeDtypeStruct((leaves, columns, points), bf16),
        in_specs=[vmem()] * 5,
        out_specs=vmem(),
        compiler_params=limit(8),
        name="down",
    )(known, other, *weights, base)
    return jnp.swapaxes(out, 1, 2)


def solution(mesh):
    placed = (
        P("leaf", None, "sub"),
        P("leaf", "sub", None, None),
        P("leaf", "sub"),
        P("leaf", None, None),
        P("leaf", None, None),
        P("leaf", "sub", None, None),
        P("leaf", "sub"),
        P("leaf", None, None),
        P("leaf", None, None),
        P("leaf", None, None, None),
        P("leaf", None),
        P("leaf", None, None),
        P("leaf", None, None),
        P(),
        P(),
        P(),
        P(),
    )
    return jax.shard_map(
        body, mesh=mesh, in_specs=placed, out_specs=P("leaf", None, "sub"), check_vma=False
    )
```

```python
import jax
import jax.numpy as jnp
from jax import lax
from jax.experimental import pallas as pl
from jax.experimental.pallas import tpu as pltpu
from jax.sharding import PartitionSpec as P

LAST = (((1,), (1,)), ((), ()))
PLAIN = (((1,), (0,)), ((), ()))


def mm(a, b, dims):
    return lax.dot_general(a, b, dims, preferred_element_type=jnp.float32)


def pinned(x, space):
    return pltpu.with_memory_space_constraint(x, space)


def limit(mebibytes):
    return pltpu.CompilerParams(vmem_limit_bytes=mebibytes * 1024 * 1024)


def vmem():
    return pl.BlockSpec(memory_space=pltpu.VMEM)


def smem():
    return pl.BlockSpec(memory_space=pltpu.SMEM)


def up_kernel(dens, col, leaf_up, node_up, coeff_out, message, dens_out):
    leaves = dens.shape[0]
    dens_out[...] = dens[...]
    coeffs = [mm(dens[t], col[t], LAST).astype(jnp.bfloat16) for t in range(leaves)]
    total = None
    for t in range(leaves):
        coeff_out[t] = coeffs[t]
        lift = mm(leaf_up[t], node_up[0], PLAIN).astype(jnp.bfloat16)
        term = mm(coeffs[t], jnp.concatenate([leaf_up[t], lift], axis=1), PLAIN)
        total = term if total is None else total + term
    message[...] = total.astype(jnp.bfloat16)


def pack_rows(pack, t, leaves, long, short):
    halves = long.shape[1] // 128
    rank = short.shape[1]
    for h in range(halves):
        pack[t * halves + h] = long[:, h * 128 : (h + 1) * 128]
    side = t % 2
    pack[leaves * halves + t // 2, :, side * rank : (side + 1) * rank] = short


def unpack_long(pack, t, halves):
    return jnp.concatenate([pack[t * halves + h] for h in range(halves)], axis=1)


def unpack_short(pack, t, leaves, halves, rank):
    side = t % 2
    return pack[leaves * halves + t // 2, :, side * rank : (side + 1) * rank]


def pack_kernel(dens, coeff, pack):
    leaves = dens.shape[0]
    for t in range(leaves):
        pack_rows(pack, t, leaves, dens[t], coeff[t])


def stage_kernel(*refs):
    count = len(refs) // 2
    sems = refs[-1]
    copies = [
        pltpu.make_async_copy(source, target, sems.at[k])
        for k, (source, target) in enumerate(zip(refs[:count], refs[count:-1]))
    ]
    for copy in copies:
        copy.start()
    for copy in copies:
        copy.wait()


def field_kernel(
    near_list, far_list, pair, own, cross, own_other, both_other, coup, near,
    near_out, far_out, send, ext, ext_coeff,
):
    leaves, entries = near.shape[0], near.shape[1]
    columns = own.shape[1]
    rank = coup.shape[-1]
    halves = near.shape[-1] // 128
    me = lax.axis_index("leaf")
    odd = me & 1
    tiles = own.shape[0]
    pair_other, cross_other = both_other.at[:tiles], both_other.at[tiles:]
    for slot, pair_of_cores in (
        (2 - 2 * odd, (pair, pair_other)),
        (1, (own, own_other)),
        (2 * odd, (cross, cross_other)),
    ):
        for c, ref in enumerate(pair_of_cores):
            rows = slice(c * columns, (c + 1) * columns)
            for t in range(leaves):
                ext[slot * leaves + t, rows] = unpack_long(ref, t, halves)
                ext_coeff[slot * leaves + t, rows] = unpack_short(ref, t, leaves, halves, rank)
    offset = (me - 1) * leaves
    for t in range(leaves):
        total = None
        for j in range(entries):
            term = mm(ext[near_list[j, t] - offset], near[t, j], LAST)
            total = term if total is None else total + term
        far = None
        for j in range(entries):
            term = mm(ext_coeff[far_list[j, t] - offset], coup[t, j], LAST)
            far = term if far is None else far + term
        near_out[t] = total[:columns]
        far_out[t] = far[:columns]
        pack_rows(
            send, t, leaves, total[columns:].astype(jnp.bfloat16), far[columns:].astype(jnp.bfloat16)
        )


def weights_kernel(
    node_list, upper_list, node_coup, node_down, upper_coup, upper_up, upper_down,
    to_field, named, *tree,
):
    nodes, rank = to_field.shape[0], to_field.shape[1]
    farc = node_coup.shape[1]
    levels = nodes.bit_length() - 1
    me = lax.axis_index("leaf")
    named[...] = jnp.zeros_like(named)
    for j in range(farc):
        place = node_list[0, j] ^ me
        named[place] = named[place] + node_coup[0, j].astype(jnp.float32)
    for height in range(1, levels):
        breadth = 2**height
        node = (nodes + me) >> (levels - height)
        level = tree[height - 1]
        level[...] = jnp.zeros_like(level)
        for j in range(farc):
            place = upper_list[j, node - 2] - breadth
            level[place] = level[place] + upper_coup[node - 2, j].astype(jnp.float32)
        if height > 1:
            for parent in range(breadth // 2):
                above = tree[height - 2][parent].astype(jnp.bfloat16)
                above = mm(upper_down[node - 4], above, PLAIN).astype(jnp.bfloat16)
                for m in (2 * parent, 2 * parent + 1):
                    level[m] = level[m] + mm(above, upper_up[breadth + m - 4], LAST)
    for parent in range(nodes // 2):
        lifted = mm(node_down[0], tree[levels - 2][parent].astype(jnp.bfloat16), PLAIN)
        lifted = lifted.astype(jnp.bfloat16)
        for n in (2 * parent, 2 * parent + 1):
            to_field[n ^ me, :, rank:] = lifted
    for place in range(nodes):
        to_field[place, :, :rank] = named[place].astype(jnp.bfloat16)


def base_kernel(near, far, received, row, leaf_down, base, to_points):
    leaves, rank = row.shape[0], row.shape[1]
    halves = near.shape[2] // 128
    for t in range(leaves):
        local = far[t] + unpack_short(received, t, leaves, halves, rank).astype(jnp.float32)
        close = near[t] + unpack_long(received, t, halves).astype(jnp.float32)
        base[t] = close + mm(local.astype(jnp.bfloat16), row[t], PLAIN)
        to_points[t] = mm(leaf_down[t], row[t], (((0,), (0,)), ((), ()))).astype(jnp.bfloat16)


def down_kernel(known, other, to_field, to_points, base, out):
    half = known.shape[0]
    messages = [known[p] for p in range(half)] + [other[p] for p in range(half)]
    matrices = [to_field[p] for p in range(2 * half)]
    field = mm(jnp.concatenate(messages, axis=1), jnp.concatenate(matrices, axis=1), LAST)
    field = field.astype(jnp.bfloat16)
    for t in range(out.shape[0]):
        out[t] = (base[t] + mm(field, to_points[t], PLAIN)).astype(jnp.bfloat16)


def body(
    density,
    near_blocks,
    near_index,
    col_basis,
    row_basis,
    leaf_coupling,
    leaf_list,
    leaf_up,
    leaf_down,
    node_coupling,
    node_list,
    node_up,
    node_down,
    upper_coupling,
    upper_list,
    upper_up,
    upper_down,
):
    leaves, points, columns = density.shape
    rank = col_basis.shape[2]
    nodes = lax.axis_size("leaf")
    levels = nodes.bit_length() - 1
    bf16, f32 = jnp.bfloat16, jnp.float32
    swap = [(0, 1), (1, 0)]

    dens = jnp.swapaxes(density, 1, 2)
    coeff, message, dens_here = pl.pallas_call(
        up_kernel,
        out_shape=(
            pltpu.VMEM((leaves, columns, rank), bf16),
            pltpu.VMEM((columns, 2 * rank), bf16),
            pltpu.VMEM(dens.shape, bf16),
        ),
        in_specs=[vmem()] * 4,
        out_specs=(vmem(),) * 3,
        compiler_params=limit(4),
        cost_estimate=pl.CostEstimate(
            flops=2_000_000_000, bytes_accessed=5_000_000, transcendentals=0
        ),
        name="up",
    )(*[pinned(x, pltpu.HBM) for x in (dens, jnp.swapaxes(col_basis, 1, 2), leaf_up, node_up)])
    tiles = leaves * (points // 128) + leaves // 2
    pack = pl.pallas_call(
        pack_kernel,
        out_shape=pltpu.VMEM((tiles, columns, 128), bf16),
        in_specs=[vmem()] * 2,
        out_specs=vmem(),
        compiler_params=limit(4),
        cost_estimate=pl.CostEstimate(
            flops=2_000_000_000, bytes_accessed=5_000_000, transcendentals=0
        ),
        name="pack",
    )(pinned(dens_here, pltpu.VMEM), pinned(coeff, pltpu.VMEM))
    staged = (near_index.T, leaf_list.T, leaf_coupling, near_blocks)
    cores = lax.axis_size("sub")
    others = [
        (i * cores + c, (i + 1 if i % 2 else i - 1) * cores + c)
        for i in range(1, nodes - 1)
        for c in range(cores)
    ]
    others += [(i * cores + c, i * cores + 1 - c) for i in (0, nodes - 1) for c in range(cores)]

    cross = lax.ppermute(pack, ("leaf", "sub"), others)
    pair = lax.ppermute(pack, "leaf", [(i, i ^ 1) for i in range(nodes)])
    own_other = lax.ppermute(pack, "sub", swap)

    entries = near_blocks.shape[1]

    def fields(*packs):
        return pl.pallas_call(
            field_kernel,
            out_shape=(
                pltpu.VMEM((leaves, columns, points), f32),
                pltpu.VMEM((leaves, columns, rank), f32),
                pltpu.VMEM((tiles, columns, 128), bf16),
            ),
            in_specs=[smem()] * 2 + [vmem()] * 7,
            out_specs=(vmem(),) * 3,
            scratch_shapes=[
                pltpu.VMEM((3 * leaves, 2 * columns, points), bf16),
                pltpu.VMEM((3 * leaves, 2 * columns, rank), bf16),
            ],
            compiler_params=limit(8),
            cost_estimate=pl.CostEstimate(
                flops=2 * leaves * entries * points * points * 256,
                bytes_accessed=leaves * entries * points * points * 2,
                transcendentals=0,
            ),
            name="fields",
        )(staged[0], staged[1], *packs, staged[2], staged[3])

    row = jnp.swapaxes(row_basis, 1, 2)
    to_field = pl.pallas_call(
        weights_kernel,
        out_shape=pltpu.VMEM((nodes, rank, 2 * rank), bf16),
        in_specs=[smem()] * 2 + [vmem()] * 5,
        out_specs=vmem(),
        scratch_shapes=[pltpu.VMEM((nodes, rank, rank), f32)]
        + [pltpu.VMEM((2**height, rank, rank), f32) for height in range(1, levels)],
        compiler_params=limit(16),
        cost_estimate=pl.CostEstimate(
            flops=2_000_000_000, bytes_accessed=3_000_000, transcendentals=0
        ),
        name="weights",
    )(
        node_list, upper_list.T, node_coupling, node_down, upper_coupling, upper_up, upper_down,
    )

    known = message[None]
    for bit in range(levels):
        step = 1 << bit
        other = lax.ppermute(known, "leaf", [(i, i ^ step) for i in range(nodes)])
        if bit == 0:
            known, other, pack = lax.optimization_barrier((known, other, pack))
        if bit == 1:
            known, other, cross, pair, own_other, to_field = lax.optimization_barrier(
                (known, other, cross, pair, own_other, to_field)
            )
            both_other = lax.ppermute(jnp.concatenate([pair, cross], axis=0), "sub", swap)
        if bit == levels - 2:
            near, far, send = fields(pair, pack, cross, own_other, both_other)
            known, other, near, far, send = lax.optimization_barrier(
                (known, other, near, far, send)
            )
        if bit < levels - 1:
            known = jnp.concatenate([known, other], axis=0)
    received = lax.ppermute(send, "sub", swap)
    base, to_points = pl.pallas_call(
        base_kernel,
        out_shape=(
            pltpu.VMEM((leaves, columns, points), f32),
            pltpu.VMEM((leaves, rank, points), bf16),
        ),
        in_specs=[vmem()] * 5,
        out_specs=(vmem(),) * 2,
        compiler_params=limit(4),
        cost_estimate=pl.CostEstimate(
            flops=1_000_000_000, bytes_accessed=1_000_000, transcendentals=0
        ),
        name="base",
    )(near, far, received, row, leaf_down)
    other, base = lax.optimization_barrier((other, base))
    out = pl.pallas_call(
        down_kernel,
        out_shape=jax.ShapeDtypeStruct((leaves, columns, points), bf16),
        in_specs=[vmem()] * 5,
        out_specs=vmem(),
        compiler_params=limit(8),
        name="down",
    )(known, other, to_field, to_points, base)
    return jnp.swapaxes(out, 1, 2)


def solution(mesh):
    placed = (
        P("leaf", None, "sub"),
        P("leaf", "sub", None, None),
        P("leaf", "sub"),
        P("leaf", None, None),
        P("leaf", None, None),
        P("leaf", "sub", None, None),
        P("leaf", "sub"),
        P("leaf", None, None),
        P("leaf", None, None),
        P("leaf", None, None, None),
        P("leaf", None),
        P("leaf", None, None),
        P("leaf", None, None),
        P(),
        P(),
        P(),
        P(),
    )
    return jax.shard_map(
        body, mesh=mesh, in_specs=placed, out_specs=P("leaf", None, "sub"), check_vma=False
    )
```

```python
import jax
import jax.numpy as jnp
from jax import lax
from jax.experimental import pallas as pl
from jax.experimental.pallas import tpu as pltpu
from jax.sharding import PartitionSpec as P

LAST = (((1,), (1,)), ((), ()))
PLAIN = (((1,), (0,)), ((), ()))


def mm(a, b, dims):
    return lax.dot_general(a, b, dims, preferred_element_type=jnp.float32)


def pinned(x, space):
    return pltpu.with_memory_space_constraint(x, space)


def limit(mebibytes):
    return pltpu.CompilerParams(vmem_limit_bytes=mebibytes * 1024 * 1024)


def vmem():
    return pl.BlockSpec(memory_space=pltpu.VMEM)


def smem():
    return pl.BlockSpec(memory_space=pltpu.SMEM)


def up_kernel(dens, col, leaf_up, node_up, coeff_out, message, dens_out):
    leaves, columns, _ = dens.shape
    rank = col.shape[1]
    dens_out[...] = dens[...]
    lift = leaf_up[...].reshape(leaves * rank, rank)
    lift = jnp.concatenate(
        [lift, mm(lift, node_up[0], PLAIN).astype(jnp.bfloat16)], axis=1
    )
    side = lax.broadcasted_iota(jnp.int32, (columns, 2 * rank), 1) < rank
    coeffs = []
    for t in range(0, leaves, 2):
        both = mm(
            jnp.concatenate([dens[t], dens[t + 1]], axis=0),
            jnp.concatenate([col[t], col[t + 1]], axis=0),
            LAST,
        ).astype(jnp.bfloat16)
        coeff_out[t] = both[:columns, :rank]
        coeff_out[t + 1] = both[columns:, rank:]
        coeffs.append(jnp.where(side, both[:columns], both[columns:]))
    message[...] = mm(jnp.concatenate(coeffs, axis=1), lift, PLAIN).astype(jnp.bfloat16)


def pack_rows(pack, t, leaves, long, short):
    halves = long.shape[1] // 128
    rank = short.shape[1]
    for h in range(halves):
        pack[t * halves + h] = long[:, h * 128 : (h + 1) * 128]
    side = t % 2
    pack[leaves * halves + t // 2, :, side * rank : (side + 1) * rank] = short


def unpack_long(pack, t, halves):
    return jnp.concatenate([pack[t * halves + h] for h in range(halves)], axis=1)


def unpack_short(pack, t, leaves, halves, rank):
    side = t % 2
    return pack[leaves * halves + t // 2, :, side * rank : (side + 1) * rank]


def pack_kernel(dens, coeff, pack):
    leaves = dens.shape[0]
    for t in range(leaves):
        pack_rows(pack, t, leaves, dens[t], coeff[t])


def stage_kernel(*refs):
    count = len(refs) // 2
    sems = refs[-1]
    copies = [
        pltpu.make_async_copy(source, target, sems.at[k])
        for k, (source, target) in enumerate(zip(refs[:count], refs[count:-1]))
    ]
    for copy in copies:
        copy.start()
    for copy in copies:
        copy.wait()


def field_kernel(
    near_list, far_list, pair, own, cross, all_other, coup, near, row,
    keep, send, ext, ext_coeff,
):
    leaves, entries = near.shape[0], near.shape[1]
    columns = own.shape[1]
    rank = coup.shape[-1]
    halves = near.shape[-1] // 128
    tiles = own.shape[0]
    me = lax.axis_index("leaf")
    odd = me & 1
    for k, (slot, ref) in enumerate(((2 - 2 * odd, pair), (2 * odd, cross), (1, own))):
        for c, part in enumerate((ref, all_other.at[k * tiles : (k + 1) * tiles])):
            rows = slice(c * columns, (c + 1) * columns)
            for t in range(leaves):
                ext[slot * leaves + t, rows] = unpack_long(part, t, halves)
                ext_coeff[slot * leaves + t, rows] = unpack_short(part, t, leaves, halves, rank)
    offset = (me - 1) * leaves
    for t in range(leaves):
        far = None
        for j in range(entries):
            term = mm(ext_coeff[far_list[j, t] - offset], coup[t, j], LAST)
            far = term if far is None else far + term
        total = mm(far.astype(jnp.bfloat16), row[t], PLAIN)
        for j in range(entries):
            total = total + mm(ext[near_list[j, t] - offset], near[t, j], LAST)
        keep[t] = total[:columns]
        send[t] = total[columns:].astype(jnp.bfloat16)


def place_of(distance, nodes):
    block = (4896 >> (4 * (distance & 3))) & 3
    return block * (nodes // 4) + (distance >> 2)


def weights_kernel(
    node_list, upper_list, node_coup, node_down, upper_coup, upper_up, upper_down, leaf_down, row,
    to_field, to_points, named, *tree,
):
    nodes, rank = to_field.shape[0], to_field.shape[1]
    farc = node_coup.shape[1]
    levels = nodes.bit_length() - 1
    me = lax.axis_index("leaf")
    for t in range(leaf_down.shape[0]):
        to_points[t] = mm(leaf_down[t], row[t], (((0,), (0,)), ((), ()))).astype(jnp.bfloat16)
    named[...] = jnp.zeros_like(named)
    for j in range(farc):
        place = place_of(node_list[0, j] ^ me, nodes)
        named[place] = named[place] + node_coup[0, j].astype(jnp.float32)
    for height in range(1, levels):
        breadth = 2**height
        node = (nodes + me) >> (levels - height)
        level = tree[height - 1]
        level[...] = jnp.zeros_like(level)
        for j in range(farc):
            place = upper_list[j, node - 2] - breadth
            level[place] = level[place] + upper_coup[node - 2, j].astype(jnp.float32)
        if height > 1:
            for parent in range(breadth // 2):
                above = tree[height - 2][parent].astype(jnp.bfloat16)
                above = mm(upper_down[node - 4], above, PLAIN).astype(jnp.bfloat16)
                for m in (2 * parent, 2 * parent + 1):
                    level[m] = level[m] + mm(above, upper_up[breadth + m - 4], LAST)
    for parent in range(nodes // 2):
        lifted = mm(node_down[0], tree[levels - 2][parent].astype(jnp.bfloat16), PLAIN)
        lifted = lifted.astype(jnp.bfloat16)
        for n in (2 * parent, 2 * parent + 1):
            to_field[place_of(n ^ me, nodes), :, rank:] = lifted
    for place in range(nodes):
        to_field[place, :, :rank] = named[place].astype(jnp.bfloat16)


def down_kernel(to_field, to_points, keep, received, *rest):
    *gathered, out = rest
    messages = [part[p] for part in gathered for p in range(part.shape[0])]
    matrices = [to_field[p] for p in range(to_field.shape[0])]
    field = mm(jnp.concatenate(messages, axis=1), jnp.concatenate(matrices, axis=1), LAST)
    field = field.astype(jnp.bfloat16)
    for t in range(out.shape[0]):
        rest = keep[t] + received[t].astype(jnp.float32)
        out[t] = (rest + mm(field, to_points[t], PLAIN)).astype(jnp.bfloat16)


def body(
    density,
    near_blocks,
    near_index,
    col_basis,
    row_basis,
    leaf_coupling,
    leaf_list,
    leaf_up,
    leaf_down,
    node_coupling,
    node_list,
    node_up,
    node_down,
    upper_coupling,
    upper_list,
    upper_up,
    upper_down,
):
    leaves, points, columns = density.shape
    rank = col_basis.shape[2]
    nodes = lax.axis_size("leaf")
    levels = nodes.bit_length() - 1
    bf16, f32 = jnp.bfloat16, jnp.float32
    swap = [(0, 1), (1, 0)]

    dens = jnp.swapaxes(density, 1, 2)
    row = jnp.swapaxes(row_basis, 1, 2)
    coeff, message, dens_here = pl.pallas_call(
        up_kernel,
        out_shape=(
            pltpu.VMEM((leaves, columns, rank), bf16),
            pltpu.VMEM((columns, 2 * rank), bf16),
            pltpu.VMEM(dens.shape, bf16),
        ),
        in_specs=[vmem()] * 4,
        out_specs=(vmem(),) * 3,
        compiler_params=limit(4),
        cost_estimate=pl.CostEstimate(
            flops=2_000_000_000, bytes_accessed=5_000_000, transcendentals=0
        ),
        name="up",
    )(*[pinned(x, pltpu.HBM) for x in (dens, jnp.swapaxes(col_basis, 1, 2), leaf_up, node_up)])
    tiles = leaves * (points // 128) + leaves // 2
    pack = pl.pallas_call(
        pack_kernel,
        out_shape=pltpu.VMEM((tiles, columns, 128), bf16),
        in_specs=[vmem()] * 2,
        out_specs=vmem(),
        compiler_params=limit(4),
        cost_estimate=pl.CostEstimate(
            flops=2_000_000_000, bytes_accessed=5_000_000, transcendentals=0
        ),
        name="pack",
    )(pinned(dens_here, pltpu.VMEM), pinned(coeff, pltpu.VMEM))
    cores = lax.axis_size("sub")
    others = [
        (i * cores + c, (i + 1 if i % 2 else i - 1) * cores + c)
        for i in range(1, nodes - 1)
        for c in range(cores)
    ]
    others += [(i * cores + c, i * cores + 1 - c) for i in (0, nodes - 1) for c in range(cores)]

    cross = lax.ppermute(pack, ("leaf", "sub"), others)
    pair = lax.ppermute(pack, "leaf", [(i, i ^ 1) for i in range(nodes)])

    entries = near_blocks.shape[1]

    def fields(*packs):
        return pl.pallas_call(
            field_kernel,
            out_shape=(
                pltpu.VMEM((leaves, columns, points), f32),
                pltpu.VMEM((leaves, columns, points), bf16),
            ),
            in_specs=[smem()] * 2 + [vmem()] * 7,
            out_specs=(vmem(),) * 2,
            scratch_shapes=[
                pltpu.VMEM((3 * leaves, 2 * columns, points), bf16),
                pltpu.VMEM((3 * leaves, 2 * columns, rank), bf16),
            ],
            compiler_params=limit(8),
            cost_estimate=pl.CostEstimate(
                flops=2 * leaves * entries * points * points * 256,
                bytes_accessed=leaves * entries * points * points * 2,
                transcendentals=0,
            ),
            name="fields",
        )(near_index.T, leaf_list.T, *packs, leaf_coupling, near_blocks, row)

    weights = pl.pallas_call(
        weights_kernel,
        out_shape=(
            pltpu.VMEM((nodes, rank, 2 * rank), bf16),
            pltpu.VMEM((leaves, rank, points), bf16),
        ),
        in_specs=[smem()] * 2 + [vmem()] * 7,
        out_specs=(vmem(),) * 2,
        scratch_shapes=[pltpu.VMEM((nodes, rank, rank), f32)]
        + [pltpu.VMEM((2**height, rank, rank), f32) for height in range(1, levels)],
        compiler_params=limit(16),
        cost_estimate=pl.CostEstimate(
            flops=2_000_000_000, bytes_accessed=3_000_000, transcendentals=0
        ),
        name="weights",
    )(
        node_list, upper_list.T, node_coupling, node_down, upper_coupling, upper_up, upper_down,
        leaf_down, row,
    )

    known = message[None]
    for bit in range(2, levels):
        step = 1 << bit
        other = lax.ppermute(known, "leaf", [(i, i ^ step) for i in range(nodes)])
        if bit == 2:
            known, other, pack = lax.optimization_barrier((known, other, pack))
        if bit == 3:
            known, other, cross, pair, weights = lax.optimization_barrier(
                (known, other, cross, pair, weights)
            )
        known = jnp.concatenate([known, other], axis=0)
    all_other = lax.ppermute(jnp.concatenate([pair, cross, pack], axis=0), "sub", swap)
    others = [
        lax.ppermute(known, "leaf", [(i, i ^ step) for i in range(nodes)]) for step in (3, 1, 2)
    ]
    keep, send = fields(pair, pack, cross, all_other)
    others, keep, send = lax.optimization_barrier((others, keep, send))
    received = lax.ppermute(send, "sub", swap)
    out = pl.pallas_call(
        down_kernel,
        out_shape=jax.ShapeDtypeStruct((leaves, columns, points), bf16),
        in_specs=[vmem()] * 8,
        out_specs=vmem(),
        compiler_params=limit(8),
        name="down",
    )(*weights, keep, received, known, *others)
    return jnp.swapaxes(out, 1, 2)


def solution(mesh):
    placed = (
        P("leaf", None, "sub"),
        P("leaf", "sub", None, None),
        P("leaf", "sub"),
        P("leaf", None, None),
        P("leaf", None, None),
        P("leaf", "sub", None, None),
        P("leaf", "sub"),
        P("leaf", None, None),
        P("leaf", None, None),
        P("leaf", None, None, None),
        P("leaf", None),
        P("leaf", None, None),
        P("leaf", None, None),
        P(),
        P(),
        P(),
        P(),
    )
    return jax.shard_map(
        body, mesh=mesh, in_specs=placed, out_specs=P("leaf", None, "sub"), check_vma=False
    )
```

```python
import jax
import jax.numpy as jnp
from jax import lax
from jax.experimental import pallas as pl
from jax.experimental.pallas import tpu as pltpu
from jax.sharding import PartitionSpec as P

LAST = (((1,), (1,)), ((), ()))
PLAIN = (((1,), (0,)), ((), ()))


def mm(a, b, dims):
    return lax.dot_general(a, b, dims, preferred_element_type=jnp.float32)


def pinned(x, space):
    return pltpu.with_memory_space_constraint(x, space)


def limit(mebibytes):
    return pltpu.CompilerParams(vmem_limit_bytes=mebibytes * 1024 * 1024)


def vmem():
    return pl.BlockSpec(memory_space=pltpu.VMEM)


def smem():
    return pl.BlockSpec(memory_space=pltpu.SMEM)


def up_kernel(dens, col, leaf_up, node_up, coeff_out, message, dens_out):
    leaves, columns, _ = dens.shape
    rank = col.shape[1]
    dens_out[...] = dens[...]
    lift = leaf_up[...].reshape(leaves * rank, rank)
    lift = jnp.concatenate(
        [lift, mm(lift, node_up[0], PLAIN).astype(jnp.bfloat16)], axis=1
    )
    side = lax.broadcasted_iota(jnp.int32, (columns, 2 * rank), 1) < rank
    coeffs = []
    for t in range(0, leaves, 2):
        both = mm(
            jnp.concatenate([dens[t], dens[t + 1]], axis=0),
            jnp.concatenate([col[t], col[t + 1]], axis=0),
            LAST,
        ).astype(jnp.bfloat16)
        coeff_out[t] = both[:columns, :rank]
        coeff_out[t + 1] = both[columns:, rank:]
        coeffs.append(jnp.where(side, both[:columns], both[columns:]))
    message[...] = mm(jnp.concatenate(coeffs, axis=1), lift, PLAIN).astype(jnp.bfloat16)


def pack_rows(pack, t, leaves, long, short):
    halves = long.shape[1] // 128
    rank = short.shape[1]
    for h in range(halves):
        pack[t * halves + h] = long[:, h * 128 : (h + 1) * 128]
    side = t % 2
    pack[leaves * halves + t // 2, :, side * rank : (side + 1) * rank] = short


def unpack_long(pack, t, halves):
    return jnp.concatenate([pack[t * halves + h] for h in range(halves)], axis=1)


def unpack_short(pack, t, leaves, halves, rank):
    side = t % 2
    return pack[leaves * halves + t // 2, :, side * rank : (side + 1) * rank]


def pack_kernel(dens, coeff, pack):
    leaves = dens.shape[0]
    for t in range(leaves):
        pack_rows(pack, t, leaves, dens[t], coeff[t])


def stage_kernel(*refs):
    count = len(refs) // 2
    sems = refs[-1]
    copies = [
        pltpu.make_async_copy(source, target, sems.at[k])
        for k, (source, target) in enumerate(zip(refs[:count], refs[count:-1]))
    ]
    for copy in copies:
        copy.start()
    for copy in copies:
        copy.wait()


def field_kernel(
    near_list, far_list, pair, own, cross, all_other, coup, near, row,
    keep, send, ext, ext_coeff,
):
    leaves, entries = near.shape[0], near.shape[1]
    columns = own.shape[1]
    rank = coup.shape[-1]
    halves = near.shape[-1] // 128
    tiles = own.shape[0]
    me = lax.axis_index("leaf")
    odd = me & 1
    for k, (slot, ref) in enumerate(((2 - 2 * odd, pair), (2 * odd, cross), (1, own))):
        for c, part in enumerate((ref, all_other.at[k * tiles : (k + 1) * tiles])):
            rows = slice(c * columns, (c + 1) * columns)
            for t in range(leaves):
                ext[slot * leaves + t, rows] = unpack_long(part, t, halves)
                ext_coeff[slot * leaves + t, rows] = unpack_short(part, t, leaves, halves, rank)
    offset = (me - 1) * leaves
    for t in range(leaves):
        far = None
        for j in range(entries):
            term = mm(ext_coeff[far_list[j, t] - offset], coup[t, j], LAST)
            far = term if far is None else far + term
        sources = [ext[near_list[j, t] - offset] for j in range(entries)]
        matrices = [near[t, j] for j in range(entries)]
        total = mm(far.astype(jnp.bfloat16), row[t], PLAIN)
        total = total + mm(
            jnp.concatenate(sources, axis=1), jnp.concatenate(matrices, axis=1), LAST
        )
        keep[t] = total[:columns]
        send[t] = total[columns:].astype(jnp.bfloat16)


def place_of(distance, nodes):
    block = (4896 >> (4 * (distance & 3))) & 3
    return block * (nodes // 4) + (distance >> 2)


def weights_kernel(
    node_list, upper_list, node_coup, node_down, upper_coup, upper_up, upper_down, leaf_down, row,
    to_field, to_points, named, *tree,
):
    nodes, rank = to_field.shape[0], to_field.shape[1]
    farc = node_coup.shape[1]
    levels = nodes.bit_length() - 1
    me = lax.axis_index("leaf")
    for t in range(leaf_down.shape[0]):
        to_points[t] = mm(leaf_down[t], row[t], (((0,), (0,)), ((), ()))).astype(jnp.bfloat16)
    named[...] = jnp.zeros_like(named)
    for j in range(farc):
        place = place_of(node_list[0, j] ^ me, nodes)
        named[place] = named[place] + node_coup[0, j].astype(jnp.float32)
    for height in range(1, levels):
        breadth = 2**height
        node = (nodes + me) >> (levels - height)
        level = tree[height - 1]
        level[...] = jnp.zeros_like(level)
        for j in range(farc):
            place = upper_list[j, node - 2] - breadth
            level[place] = level[place] + upper_coup[node - 2, j].astype(jnp.float32)
        if height > 1:
            for parent in range(breadth // 2):
                above = tree[height - 2][parent].astype(jnp.bfloat16)
                above = mm(upper_down[node - 4], above, PLAIN).astype(jnp.bfloat16)
                for m in (2 * parent, 2 * parent + 1):
                    level[m] = level[m] + mm(above, upper_up[breadth + m - 4], LAST)
    for parent in range(nodes // 2):
        lifted = mm(node_down[0], tree[levels - 2][parent].astype(jnp.bfloat16), PLAIN)
        lifted = lifted.astype(jnp.bfloat16)
        for n in (2 * parent, 2 * parent + 1):
            to_field[place_of(n ^ me, nodes), :, rank:] = lifted
    for place in range(nodes):
        to_field[place, :, :rank] = named[place].astype(jnp.bfloat16)


def down_kernel(to_field, to_points, keep, *rest):
    *gathered, out = rest
    messages = [part[p] for part in gathered for p in range(part.shape[0])]
    matrices = [to_field[p] for p in range(to_field.shape[0])]
    field = mm(jnp.concatenate(messages, axis=1), jnp.concatenate(matrices, axis=1), LAST)
    field = field.astype(jnp.bfloat16)
    for t in range(out.shape[0]):
        out[t] = keep[t] + mm(field, to_points[t], PLAIN)


def body(
    density,
    near_blocks,
    near_index,
    col_basis,
    row_basis,
    leaf_coupling,
    leaf_list,
    leaf_up,
    leaf_down,
    node_coupling,
    node_list,
    node_up,
    node_down,
    upper_coupling,
    upper_list,
    upper_up,
    upper_down,
):
    leaves, points, columns = density.shape
    rank = col_basis.shape[2]
    nodes = lax.axis_size("leaf")
    levels = nodes.bit_length() - 1
    bf16, f32 = jnp.bfloat16, jnp.float32
    swap = [(0, 1), (1, 0)]

    dens = jnp.swapaxes(density, 1, 2)
    row = jnp.swapaxes(row_basis, 1, 2)
    coeff, message, dens_here = pl.pallas_call(
        up_kernel,
        out_shape=(
            pltpu.VMEM((leaves, columns, rank), bf16),
            pltpu.VMEM((columns, 2 * rank), bf16),
            pltpu.VMEM(dens.shape, bf16),
        ),
        in_specs=[vmem()] * 4,
        out_specs=(vmem(),) * 3,
        compiler_params=limit(4),
        cost_estimate=pl.CostEstimate(
            flops=2_000_000_000, bytes_accessed=5_000_000, transcendentals=0
        ),
        name="up",
    )(*[pinned(x, pltpu.HBM) for x in (dens, jnp.swapaxes(col_basis, 1, 2), leaf_up, node_up)])
    tiles = leaves * (points // 128) + leaves // 2
    pack = pl.pallas_call(
        pack_kernel,
        out_shape=pltpu.VMEM((tiles, columns, 128), bf16),
        in_specs=[vmem()] * 2,
        out_specs=vmem(),
        compiler_params=limit(4),
        cost_estimate=pl.CostEstimate(
            flops=2_000_000_000, bytes_accessed=5_000_000, transcendentals=0
        ),
        name="pack",
    )(pinned(dens_here, pltpu.VMEM), pinned(coeff, pltpu.VMEM))
    cores = lax.axis_size("sub")
    others = [
        (i * cores + c, (i + 1 if i % 2 else i - 1) * cores + c)
        for i in range(1, nodes - 1)
        for c in range(cores)
    ]
    others += [(i * cores + c, i * cores + 1 - c) for i in (0, nodes - 1) for c in range(cores)]

    cross = lax.ppermute(pack, ("leaf", "sub"), others)
    pair = lax.ppermute(pack, "leaf", [(i, i ^ 1) for i in range(nodes)])

    entries = near_blocks.shape[1]

    def fields(*packs):
        return pl.pallas_call(
            field_kernel,
            out_shape=(
                pltpu.VMEM((leaves, columns, points), f32),
                pltpu.VMEM((leaves, columns, points), bf16),
            ),
            in_specs=[smem()] * 2 + [vmem()] * 7,
            out_specs=(vmem(),) * 2,
            scratch_shapes=[
                pltpu.VMEM((3 * leaves, 2 * columns, points), bf16),
                pltpu.VMEM((3 * leaves, 2 * columns, rank), bf16),
            ],
            compiler_params=limit(8),
            cost_estimate=pl.CostEstimate(
                flops=2 * leaves * entries * points * points * 256,
                bytes_accessed=leaves * entries * points * points * 2,
                transcendentals=0,
            ),
            name="fields",
        )(near_index.T, leaf_list.T, *packs, leaf_coupling, near_blocks, row)

    weights = pl.pallas_call(
        weights_kernel,
        out_shape=(
            pltpu.VMEM((nodes, rank, 2 * rank), bf16),
            pltpu.VMEM((leaves, rank, points), bf16),
        ),
        in_specs=[smem()] * 2 + [vmem()] * 7,
        out_specs=(vmem(),) * 2,
        scratch_shapes=[pltpu.VMEM((nodes, rank, rank), f32)]
        + [pltpu.VMEM((2**height, rank, rank), f32) for height in range(1, levels)],
        compiler_params=limit(16),
        cost_estimate=pl.CostEstimate(
            flops=2_000_000_000, bytes_accessed=3_000_000, transcendentals=0
        ),
        name="weights",
    )(
        node_list, upper_list.T, node_coupling, node_down, upper_coupling, upper_up, upper_down,
        leaf_down, row,
    )

    known = message[None]
    for bit in range(2, levels):
        step = 1 << bit
        other = lax.ppermute(known, "leaf", [(i, i ^ step) for i in range(nodes)])
        if bit == 2:
            known, other, pack = lax.optimization_barrier((known, other, pack))
        if bit == 3:
            known, other, cross, pair, weights = lax.optimization_barrier(
                (known, other, cross, pair, weights)
            )
        known = jnp.concatenate([known, other], axis=0)
    all_other = lax.ppermute(jnp.concatenate([pair, cross, pack], axis=0), "sub", swap)
    others = [
        lax.ppermute(known, "leaf", [(i, i ^ step) for i in range(nodes)]) for step in (3, 1, 2)
    ]
    keep, send = fields(pair, pack, cross, all_other)
    others, keep, send = lax.optimization_barrier((others, keep, send))
    received = lax.ppermute(send, "sub", swap)
    part = pl.pallas_call(
        down_kernel,
        out_shape=pltpu.VMEM((leaves, columns, points), f32),
        in_specs=[vmem()] * 7,
        out_specs=vmem(),
        compiler_params=limit(8),
        cost_estimate=pl.CostEstimate(
            flops=1_000_000_000, bytes_accessed=1_000_000, transcendentals=0
        ),
        name="down",
    )(*weights, keep, known, *others)
    out = (part + received.astype(f32)).astype(bf16)
    return jnp.swapaxes(out, 1, 2)


def solution(mesh):
    placed = (
        P("leaf", None, "sub"),
        P("leaf", "sub", None, None),
        P("leaf", "sub"),
        P("leaf", None, None),
        P("leaf", None, None),
        P("leaf", "sub", None, None),
        P("leaf", "sub"),
        P("leaf", None, None),
        P("leaf", None, None),
        P("leaf", None, None, None),
        P("leaf", None),
        P("leaf", None, None),
        P("leaf", None, None),
        P(),
        P(),
        P(),
        P(),
    )
    return jax.shard_map(
        body, mesh=mesh, in_specs=placed, out_specs=P("leaf", None, "sub"), check_vma=False
    )
```

```python
import jax
import jax.numpy as jnp
from jax import lax
from jax.experimental import pallas as pl
from jax.experimental.pallas import tpu as pltpu
from jax.sharding import PartitionSpec as P

LAST = (((1,), (1,)), ((), ()))
PLAIN = (((1,), (0,)), ((), ()))


def mm(a, b, dims):
    return lax.dot_general(a, b, dims, preferred_element_type=jnp.float32)


def pinned(x, space):
    return pltpu.with_memory_space_constraint(x, space)


def limit(mebibytes):
    return pltpu.CompilerParams(vmem_limit_bytes=mebibytes * 1024 * 1024)


def vmem():
    return pl.BlockSpec(memory_space=pltpu.VMEM)


def smem():
    return pl.BlockSpec(memory_space=pltpu.SMEM)


def up_kernel(dens, col, leaf_up, node_up, coeff_out, message, dens_out):
    leaves, columns, _ = dens.shape
    rank = col.shape[1]
    dens_out[...] = dens[...]
    lift = leaf_up[...].reshape(leaves * rank, rank)
    lift = jnp.concatenate(
        [lift, mm(lift, node_up[0], PLAIN).astype(jnp.bfloat16)], axis=1
    )
    side = lax.broadcasted_iota(jnp.int32, (columns, 2 * rank), 1) < rank
    coeffs = []
    for t in range(0, leaves, 2):
        both = mm(
            jnp.concatenate([dens[t], dens[t + 1]], axis=0),
            jnp.concatenate([col[t], col[t + 1]], axis=0),
            LAST,
        ).astype(jnp.bfloat16)
        coeff_out[t] = both[:columns, :rank]
        coeff_out[t + 1] = both[columns:, rank:]
        coeffs.append(jnp.where(side, both[:columns], both[columns:]))
    message[...] = mm(jnp.concatenate(coeffs, axis=1), lift, PLAIN).astype(jnp.bfloat16)


def pack_rows(pack, t, leaves, long, short):
    halves = long.shape[1] // 128
    rank = short.shape[1]
    for h in range(halves):
        pack[t * halves + h] = long[:, h * 128 : (h + 1) * 128]
    side = t % 2
    pack[leaves * halves + t // 2, :, side * rank : (side + 1) * rank] = short


def unpack_long(pack, t, halves):
    return jnp.concatenate([pack[t * halves + h] for h in range(halves)], axis=1)


def unpack_short(pack, t, leaves, halves, rank):
    side = t % 2
    return pack[leaves * halves + t // 2, :, side * rank : (side + 1) * rank]


def pack_kernel(dens, coeff, pack):
    leaves = dens.shape[0]
    for t in range(leaves):
        pack_rows(pack, t, leaves, dens[t], coeff[t])


def stage_kernel(*refs):
    count = len(refs) // 2
    sems = refs[-1]
    copies = [
        pltpu.make_async_copy(source, target, sems.at[k])
        for k, (source, target) in enumerate(zip(refs[:count], refs[count:-1]))
    ]
    for copy in copies:
        copy.start()
    for copy in copies:
        copy.wait()


def field_kernel(
    near_list, far_list, pair, own, cross, all_other, coup, near, row,
    keep, send, ext, ext_coeff,
):
    leaves, entries = near.shape[0], near.shape[1]
    columns = own.shape[1]
    rank = coup.shape[-1]
    halves = near.shape[-1] // 128
    tiles = own.shape[0]
    me = lax.axis_index("leaf")
    odd = me & 1
    for k, (slot, ref) in enumerate(((2 - 2 * odd, pair), (2 * odd, cross), (1, own))):
        for c, part in enumerate((ref, all_other.at[k * tiles : (k + 1) * tiles])):
            rows = slice(c * columns, (c + 1) * columns)
            for t in range(leaves):
                ext[slot * leaves + t, rows] = unpack_long(part, t, halves)
                ext_coeff[slot * leaves + t, rows] = unpack_short(part, t, leaves, halves, rank)
    offset = (me - 1) * leaves
    for t in range(leaves):
        far = None
        for j in range(entries):
            term = mm(ext_coeff[far_list[j, t] - offset], coup[t, j], LAST)
            far = term if far is None else far + term
        sources = [ext[near_list[j, t] - offset] for j in range(entries)]
        matrices = [near[t, j] for j in range(entries)]
        total = mm(far.astype(jnp.bfloat16), row[t], PLAIN)
        total = total + mm(
            jnp.concatenate(sources, axis=1), jnp.concatenate(matrices, axis=1), LAST
        )
        keep[t] = total[:columns]
        send[t] = total[columns:].astype(jnp.bfloat16)


def place_of(distance, nodes):
    block = (4896 >> (4 * (distance & 3))) & 3
    return block * (nodes // 4) + (distance >> 2)


def weights_kernel(
    node_list, upper_list, node_coup, upper_coup, upper_up, upper_down, leaf_down, row,
    to_field, to_points, named, *tree,
):
    nodes, rank = to_field.shape[0], row.shape[1]
    farc = node_coup.shape[1]
    levels = nodes.bit_length() - 1
    me = lax.axis_index("leaf")
    for t in range(leaf_down.shape[0]):
        to_points[t] = mm(leaf_down[t], row[t], (((0,), (0,)), ((), ()))).astype(jnp.bfloat16)
    named[...] = jnp.zeros_like(named)
    for j in range(farc):
        place = place_of(node_list[0, j] ^ me, nodes)
        named[place] = named[place] + node_coup[0, j].astype(jnp.float32)
    for height in range(1, levels):
        breadth = 2**height
        node = (nodes + me) >> (levels - height)
        level = tree[height - 1]
        level[...] = jnp.zeros_like(level)
        for j in range(farc):
            place = upper_list[j, node - 2] - breadth
            level[place] = level[place] + upper_coup[node - 2, j].astype(jnp.float32)
        if height > 1:
            for parent in range(breadth // 2):
                above = tree[height - 2][parent].astype(jnp.bfloat16)
                above = mm(upper_down[node - 4], above, PLAIN).astype(jnp.bfloat16)
                first = breadth + 2 * parent - 4
                pair = mm(above, upper_up[first : first + 2].reshape(2 * rank, rank), LAST)
                for side in range(2):
                    m = 2 * parent + side
                    level[m] = level[m] + pair[:, side * rank : (side + 1) * rank]
    blank = jnp.zeros((rank, rank), jnp.bfloat16)
    for place in range(nodes):
        block = jnp.concatenate([named[place].astype(jnp.bfloat16), blank], axis=1)
        to_field[place, :rank] = block
    for parent in range(nodes // 2):
        composed = tree[levels - 2][parent].astype(jnp.bfloat16)
        composed = jnp.concatenate([blank, composed], axis=1)
        for n in (2 * parent, 2 * parent + 1):
            to_field[place_of(n ^ me, nodes), rank:] = composed


def down_kernel(to_field, to_points, node_down, keep, *rest):
    *gathered, out = rest
    messages = [part[p] for part in gathered for p in range(part.shape[0])]
    matrices = [to_field[p] for p in range(to_field.shape[0])]
    fields = mm(jnp.concatenate(messages, axis=1), jnp.concatenate(matrices, axis=1), LAST)
    rank = node_down.shape[-1]
    parent = fields[:, rank:].astype(jnp.bfloat16)
    field = (fields[:, :rank] + mm(parent, node_down[0], LAST)).astype(jnp.bfloat16)
    for t in range(out.shape[0]):
        out[t] = keep[t] + mm(field, to_points[t], PLAIN)


def body(
    density,
    near_blocks,
    near_index,
    col_basis,
    row_basis,
    leaf_coupling,
    leaf_list,
    leaf_up,
    leaf_down,
    node_coupling,
    node_list,
    node_up,
    node_down,
    upper_coupling,
    upper_list,
    upper_up,
    upper_down,
):
    leaves, points, columns = density.shape
    rank = col_basis.shape[2]
    nodes = lax.axis_size("leaf")
    levels = nodes.bit_length() - 1
    bf16, f32 = jnp.bfloat16, jnp.float32
    swap = [(0, 1), (1, 0)]

    dens = jnp.swapaxes(density, 1, 2)
    row = jnp.swapaxes(row_basis, 1, 2)
    coeff, message, dens_here = pl.pallas_call(
        up_kernel,
        out_shape=(
            pltpu.VMEM((leaves, columns, rank), bf16),
            pltpu.VMEM((columns, 2 * rank), bf16),
            pltpu.VMEM(dens.shape, bf16),
        ),
        in_specs=[vmem()] * 4,
        out_specs=(vmem(),) * 3,
        compiler_params=limit(4),
        cost_estimate=pl.CostEstimate(
            flops=2_000_000_000, bytes_accessed=5_000_000, transcendentals=0
        ),
        name="up",
    )(*[pinned(x, pltpu.HBM) for x in (dens, jnp.swapaxes(col_basis, 1, 2), leaf_up, node_up)])
    tiles = leaves * (points // 128) + leaves // 2
    pack = pl.pallas_call(
        pack_kernel,
        out_shape=pltpu.VMEM((tiles, columns, 128), bf16),
        in_specs=[vmem()] * 2,
        out_specs=vmem(),
        compiler_params=limit(4),
        cost_estimate=pl.CostEstimate(
            flops=2_000_000_000, bytes_accessed=5_000_000, transcendentals=0
        ),
        name="pack",
    )(pinned(dens_here, pltpu.VMEM), pinned(coeff, pltpu.VMEM))
    cores = lax.axis_size("sub")
    others = [
        (i * cores + c, (i + 1 if i % 2 else i - 1) * cores + c)
        for i in range(1, nodes - 1)
        for c in range(cores)
    ]
    others += [(i * cores + c, i * cores + 1 - c) for i in (0, nodes - 1) for c in range(cores)]

    cross = lax.ppermute(pack, ("leaf", "sub"), others)
    pair = lax.ppermute(pack, "leaf", [(i, i ^ 1) for i in range(nodes)])

    entries = near_blocks.shape[1]

    def fields(*packs):
        return pl.pallas_call(
            field_kernel,
            out_shape=(
                pltpu.VMEM((leaves, columns, points), f32),
                pltpu.VMEM((leaves, columns, points), bf16),
            ),
            in_specs=[smem()] * 2 + [vmem()] * 7,
            out_specs=(vmem(),) * 2,
            scratch_shapes=[
                pltpu.VMEM((3 * leaves, 2 * columns, points), bf16),
                pltpu.VMEM((3 * leaves, 2 * columns, rank), bf16),
            ],
            compiler_params=limit(8),
            cost_estimate=pl.CostEstimate(
                flops=2 * leaves * entries * points * points * 256,
                bytes_accessed=leaves * entries * points * points * 2,
                transcendentals=0,
            ),
            name="fields",
        )(near_index.T, leaf_list.T, *packs, leaf_coupling, near_blocks, row)

    weights = pl.pallas_call(
        weights_kernel,
        out_shape=(
            pltpu.VMEM((nodes, 2 * rank, 2 * rank), bf16),
            pltpu.VMEM((leaves, rank, points), bf16),
        ),
        in_specs=[smem()] * 2 + [vmem()] * 6,
        out_specs=(vmem(),) * 2,
        scratch_shapes=[pltpu.VMEM((nodes, rank, rank), f32)]
        + [pltpu.VMEM((2**height, rank, rank), f32) for height in range(1, levels)],
        compiler_params=limit(16),
        cost_estimate=pl.CostEstimate(
            flops=2_000_000_000, bytes_accessed=3_000_000, transcendentals=0
        ),
        name="weights",
    )(
        node_list, upper_list.T, node_coupling, upper_coupling, upper_up, upper_down,
        leaf_down, row,
    )

    known = message[None]
    for bit in range(2, levels):
        step = 1 << bit
        other = lax.ppermute(known, "leaf", [(i, i ^ step) for i in range(nodes)])
        if bit == 2:
            known, other, pack = lax.optimization_barrier((known, other, pack))
        if bit == 3:
            known, other, cross, pair, weights = lax.optimization_barrier(
                (known, other, cross, pair, weights)
            )
        known = jnp.concatenate([known, other], axis=0)
    all_other = lax.ppermute(jnp.concatenate([pair, cross, pack], axis=0), "sub", swap)
    others = [
        lax.ppermute(known, "leaf", [(i, i ^ step) for i in range(nodes)]) for step in (3, 1, 2)
    ]
    keep, send = fields(pair, pack, cross, all_other)
    others, keep, send = lax.optimization_barrier((others, keep, send))
    received = lax.ppermute(send, "sub", swap)
    part = pl.pallas_call(
        down_kernel,
        out_shape=pltpu.VMEM((leaves, columns, points), f32),
        in_specs=[vmem()] * 8,
        out_specs=vmem(),
        compiler_params=limit(8),
        cost_estimate=pl.CostEstimate(
            flops=1_000_000_000, bytes_accessed=1_000_000, transcendentals=0
        ),
        name="down",
    )(*weights, node_down, keep, known, *others)
    out = (part + received.astype(f32)).astype(bf16)
    return jnp.swapaxes(out, 1, 2)


def solution(mesh):
    placed = (
        P("leaf", None, "sub"),
        P("leaf", "sub", None, None),
        P("leaf", "sub"),
        P("leaf", None, None),
        P("leaf", None, None),
        P("leaf", "sub", None, None),
        P("leaf", "sub"),
        P("leaf", None, None),
        P("leaf", None, None),
        P("leaf", None, None, None),
        P("leaf", None),
        P("leaf", None, None),
        P("leaf", None, None),
        P(),
        P(),
        P(),
        P(),
    )
    return jax.shard_map(
        body, mesh=mesh, in_specs=placed, out_specs=P("leaf", None, "sub"), check_vma=False
    )
```

```python
import jax
import jax.numpy as jnp
from jax import lax
from jax.experimental import pallas as pl
from jax.experimental.pallas import tpu as pltpu
from jax.sharding import PartitionSpec as P

LAST = (((1,), (1,)), ((), ()))
PLAIN = (((1,), (0,)), ((), ()))


def mm(a, b, dims):
    return lax.dot_general(a, b, dims, preferred_element_type=jnp.float32)


def pinned(x, space):
    return pltpu.with_memory_space_constraint(x, space)


def limit(mebibytes):
    return pltpu.CompilerParams(vmem_limit_bytes=mebibytes * 1024 * 1024)


def vmem():
    return pl.BlockSpec(memory_space=pltpu.VMEM)


def smem():
    return pl.BlockSpec(memory_space=pltpu.SMEM)


def up_kernel(dens, col, leaf_up, node_up, coeff_out, message, dens_out):
    leaves, columns, _ = dens.shape
    rank = col.shape[1]
    dens_out[...] = dens[...]
    lift = leaf_up[...].reshape(leaves * rank, rank)
    lift = jnp.concatenate(
        [lift, mm(lift, node_up[0], PLAIN).astype(jnp.bfloat16)], axis=1
    )
    side = lax.broadcasted_iota(jnp.int32, (columns, 2 * rank), 1) < rank
    coeffs = []
    for t in range(0, leaves, 2):
        both = mm(
            jnp.concatenate([dens[t], dens[t + 1]], axis=0),
            jnp.concatenate([col[t], col[t + 1]], axis=0),
            LAST,
        ).astype(jnp.bfloat16)
        coeff_out[t] = both[:columns, :rank]
        coeff_out[t + 1] = both[columns:, rank:]
        coeffs.append(jnp.where(side, both[:columns], both[columns:]))
    message[...] = mm(jnp.concatenate(coeffs, axis=1), lift, PLAIN).astype(jnp.bfloat16)


def pack_rows(pack, t, leaves, long, short):
    halves = long.shape[1] // 128
    rank = short.shape[1]
    for h in range(halves):
        pack[t * halves + h] = long[:, h * 128 : (h + 1) * 128]
    side = t % 2
    pack[leaves * halves + t // 2, :, side * rank : (side + 1) * rank] = short


def unpack_long(pack, t, halves):
    return jnp.concatenate([pack[t * halves + h] for h in range(halves)], axis=1)


def unpack_short(pack, t, leaves, halves, rank):
    side = t % 2
    return pack[leaves * halves + t // 2, :, side * rank : (side + 1) * rank]


def pack_kernel(dens, coeff, pack):
    leaves = dens.shape[0]
    for t in range(leaves):
        pack_rows(pack, t, leaves, dens[t], coeff[t])


def stage_kernel(*refs):
    count = len(refs) // 2
    sems = refs[-1]
    copies = [
        pltpu.make_async_copy(source, target, sems.at[k])
        for k, (source, target) in enumerate(zip(refs[:count], refs[count:-1]))
    ]
    for copy in copies:
        copy.start()
    for copy in copies:
        copy.wait()


def field_kernel(
    near_list, far_list, pair, own, cross, all_other, coup, near, row,
    keep, send, ext, ext_coeff,
):
    leaves, entries = near.shape[0], near.shape[1]
    columns = own.shape[1]
    rank = coup.shape[-1]
    halves = near.shape[-1] // 128
    tiles = own.shape[0]
    me = lax.axis_index("leaf")
    odd = me & 1
    for k, (slot, ref) in enumerate(((2 - 2 * odd, pair), (2 * odd, cross), (1, own))):
        for c, part in enumerate((ref, all_other.at[k * tiles : (k + 1) * tiles])):
            rows = slice(c * columns, (c + 1) * columns)
            for t in range(leaves):
                ext[slot * leaves + t, rows] = unpack_long(part, t, halves)
                ext_coeff[slot * leaves + t, rows] = unpack_short(part, t, leaves, halves, rank)
    offset = (me - 1) * leaves
    for t in range(leaves):
        far = None
        for j in range(entries):
            term = mm(ext_coeff[far_list[j, t] - offset], coup[t, j], LAST)
            far = term if far is None else far + term
        sources = [ext[near_list[j, t] - offset] for j in range(entries)]
        matrices = [near[t, j] for j in range(entries)]
        total = mm(far.astype(jnp.bfloat16), row[t], PLAIN)
        total = total + mm(
            jnp.concatenate(sources, axis=1), jnp.concatenate(matrices, axis=1), LAST
        )
        keep[t] = total[:columns]
        send[t] = total[columns:].astype(jnp.bfloat16)


def place_of(distance, nodes):
    block = (8976 >> (4 * (distance & 3))) & 3
    return block * (nodes // 4) + (distance >> 2)


def weights_kernel(
    node_list, upper_list, node_coup, upper_coup, upper_up, upper_down, leaf_down, row,
    to_field, to_points, named, *tree,
):
    nodes, rank = to_field.shape[0], row.shape[1]
    farc = node_coup.shape[1]
    levels = nodes.bit_length() - 1
    me = lax.axis_index("leaf")
    for t in range(leaf_down.shape[0]):
        to_points[t] = mm(leaf_down[t], row[t], (((0,), (0,)), ((), ()))).astype(jnp.bfloat16)
    named[...] = jnp.zeros_like(named)
    for j in range(farc):
        place = place_of(node_list[0, j] ^ me, nodes)
        named[place] = named[place] + node_coup[0, j].astype(jnp.float32)
    for height in range(1, levels):
        breadth = 2**height
        node = (nodes + me) >> (levels - height)
        level = tree[height - 1]
        level[...] = jnp.zeros_like(level)
        for j in range(farc):
            place = upper_list[j, node - 2] - breadth
            level[place] = level[place] + upper_coup[node - 2, j].astype(jnp.float32)
        if height > 1:
            for parent in range(breadth // 2):
                above = tree[height - 2][parent].astype(jnp.bfloat16)
                above = mm(upper_down[node - 4], above, PLAIN).astype(jnp.bfloat16)
                first = breadth + 2 * parent - 4
                pair = mm(above, upper_up[first : first + 2].reshape(2 * rank, rank), LAST)
                for side in range(2):
                    m = 2 * parent + side
                    level[m] = level[m] + pair[:, side * rank : (side + 1) * rank]
    blank = jnp.zeros((rank, rank), jnp.bfloat16)
    for place in range(nodes):
        block = jnp.concatenate([named[place].astype(jnp.bfloat16), blank], axis=1)
        to_field[place, :rank] = block
    for parent in range(nodes // 2):
        composed = tree[levels - 2][parent].astype(jnp.bfloat16)
        composed = jnp.concatenate([blank, composed], axis=1)
        for n in (2 * parent, 2 * parent + 1):
            to_field[place_of(n ^ me, nodes), rank:] = composed


def down_kernel(to_field, to_points, node_down, keep, *rest):
    *gathered, out = rest
    messages = [part[p] for part in gathered for p in range(part.shape[0])]
    matrices = [to_field[p] for p in range(to_field.shape[0])]
    fields = mm(jnp.concatenate(messages, axis=1), jnp.concatenate(matrices, axis=1), LAST)
    rank = node_down.shape[-1]
    parent = fields[:, rank:].astype(jnp.bfloat16)
    field = (fields[:, :rank] + mm(parent, node_down[0], LAST)).astype(jnp.bfloat16)
    for t in range(out.shape[0]):
        out[t] = keep[t] + mm(field, to_points[t], PLAIN)


def body(
    density,
    near_blocks,
    near_index,
    col_basis,
    row_basis,
    leaf_coupling,
    leaf_list,
    leaf_up,
    leaf_down,
    node_coupling,
    node_list,
    node_up,
    node_down,
    upper_coupling,
    upper_list,
    upper_up,
    upper_down,
):
    leaves, points, columns = density.shape
    rank = col_basis.shape[2]
    nodes = lax.axis_size("leaf")
    levels = nodes.bit_length() - 1
    bf16, f32 = jnp.bfloat16, jnp.float32
    swap = [(0, 1), (1, 0)]

    dens = jnp.swapaxes(density, 1, 2)
    row = jnp.swapaxes(row_basis, 1, 2)
    coeff, message, dens_here = pl.pallas_call(
        up_kernel,
        out_shape=(
            pltpu.VMEM((leaves, columns, rank), bf16),
            pltpu.VMEM((columns, 2 * rank), bf16),
            pltpu.VMEM(dens.shape, bf16),
        ),
        in_specs=[vmem()] * 4,
        out_specs=(vmem(),) * 3,
        compiler_params=limit(4),
        cost_estimate=pl.CostEstimate(
            flops=2_000_000_000, bytes_accessed=5_000_000, transcendentals=0
        ),
        name="up",
    )(*[pinned(x, pltpu.HBM) for x in (dens, jnp.swapaxes(col_basis, 1, 2), leaf_up, node_up)])
    tiles = leaves * (points // 128) + leaves // 2
    pack = pl.pallas_call(
        pack_kernel,
        out_shape=pltpu.VMEM((tiles, columns, 128), bf16),
        in_specs=[vmem()] * 2,
        out_specs=vmem(),
        compiler_params=limit(4),
        cost_estimate=pl.CostEstimate(
            flops=2_000_000_000, bytes_accessed=5_000_000, transcendentals=0
        ),
        name="pack",
    )(pinned(dens_here, pltpu.VMEM), pinned(coeff, pltpu.VMEM))
    cores = lax.axis_size("sub")
    others = [
        (i * cores + c, (i + 1 if i % 2 else i - 1) * cores + c)
        for i in range(1, nodes - 1)
        for c in range(cores)
    ]
    others += [(i * cores + c, i * cores + 1 - c) for i in (0, nodes - 1) for c in range(cores)]

    cross = lax.ppermute(pack, ("leaf", "sub"), others)
    pair = lax.ppermute(pack, "leaf", [(i, i ^ 1) for i in range(nodes)])

    entries = near_blocks.shape[1]

    def fields(*packs):
        return pl.pallas_call(
            field_kernel,
            out_shape=(
                pltpu.VMEM((leaves, columns, points), f32),
                pltpu.VMEM((leaves, columns, points), bf16),
            ),
            in_specs=[smem()] * 2 + [vmem()] * 7,
            out_specs=(vmem(),) * 2,
            scratch_shapes=[
                pltpu.VMEM((3 * leaves, 2 * columns, points), bf16),
                pltpu.VMEM((3 * leaves, 2 * columns, rank), bf16),
            ],
            compiler_params=limit(8),
            cost_estimate=pl.CostEstimate(
                flops=2 * leaves * entries * points * points * 256,
                bytes_accessed=leaves * entries * points * points * 2,
                transcendentals=0,
            ),
            name="fields",
        )(near_index.T, leaf_list.T, *packs, leaf_coupling, near_blocks, row)

    weights = pl.pallas_call(
        weights_kernel,
        out_shape=(
            pltpu.VMEM((nodes, 2 * rank, 2 * rank), bf16),
            pltpu.VMEM((leaves, rank, points), bf16),
        ),
        in_specs=[smem()] * 2 + [vmem()] * 6,
        out_specs=(vmem(),) * 2,
        scratch_shapes=[pltpu.VMEM((nodes, rank, rank), f32)]
        + [pltpu.VMEM((2**height, rank, rank), f32) for height in range(1, levels)],
        compiler_params=limit(16),
        cost_estimate=pl.CostEstimate(
            flops=2_000_000_000, bytes_accessed=3_000_000, transcendentals=0
        ),
        name="weights",
    )(
        node_list, upper_list.T, node_coupling, upper_coupling, upper_up, upper_down,
        leaf_down, row,
    )

    known = message[None]
    for bit in range(2, levels):
        step = 1 << bit
        other = lax.ppermute(known, "leaf", [(i, i ^ step) for i in range(nodes)])
        if bit == 2:
            known, other, pack = lax.optimization_barrier((known, other, pack))
        if bit == 3:
            known, other, cross, pair, weights = lax.optimization_barrier(
                (known, other, cross, pair, weights)
            )
        known = jnp.concatenate([known, other], axis=0)
    all_other = lax.ppermute(jnp.concatenate([pair, cross, pack], axis=0), "sub", swap)
    others = [
        lax.ppermute(known, "leaf", [(i, i ^ step) for i in range(nodes)]) for step in (1, 3, 2)
    ]
    keep, send = fields(pair, pack, cross, all_other)
    others, keep, send = lax.optimization_barrier((others, keep, send))
    received = lax.ppermute(send, "sub", swap)
    part = pl.pallas_call(
        down_kernel,
        out_shape=pltpu.VMEM((leaves, columns, points), f32),
        in_specs=[vmem()] * 8,
        out_specs=vmem(),
        compiler_params=limit(8),
        cost_estimate=pl.CostEstimate(
            flops=1_000_000_000, bytes_accessed=1_000_000, transcendentals=0
        ),
        name="down",
    )(*weights, node_down, keep, known, *others)
    out = (part + received.astype(f32)).astype(bf16)
    return jnp.swapaxes(out, 1, 2)


def solution(mesh):
    placed = (
        P("leaf", None, "sub"),
        P("leaf", "sub", None, None),
        P("leaf", "sub"),
        P("leaf", None, None),
        P("leaf", None, None),
        P("leaf", "sub", None, None),
        P("leaf", "sub"),
        P("leaf", None, None),
        P("leaf", None, None),
        P("leaf", None, None, None),
        P("leaf", None),
        P("leaf", None, None),
        P("leaf", None, None),
        P(),
        P(),
        P(),
        P(),
    )
    return jax.shard_map(
        body, mesh=mesh, in_specs=placed, out_specs=P("leaf", None, "sub"), check_vma=False
    )
```
